32 devices in a mesh: parts: 16 (over z, y, x), pair: 2 (over core).
Axes of the slice: x: 2, y: 2, z: 4, core: 2. Of those that a mesh axis runs over, the one named last changes fastest.
Arguments:
- pulse_rhs: float32 [32, 65536], P(None, ('parts', 'pair')), may hold values from -6 to 6
- blocks_fine: float32 [512, 4, 128, 128], P(('parts', 'pair'))
- columns_fine: int32 [512, 4], P(('parts', 'pair')), may hold values from 0 to 19, as said below
- aggregate_fine: int32 [65536], P(('parts', 'pair')), may hold values from 0 to 127
- blocks_mid: float32 [128, 4, 128, 128], P(('parts', 'pair'))
- columns_mid: int32 [128, 4], P(('parts', 'pair')), may hold values from 0 to 7, as said below
- aggregate_mid: int32 [16384], P(('parts', 'pair')), may hold values from 0 to 127
- blocks_low: float32 [64, 4, 128, 128], P(('parts', 'pair'))
- columns_low: int32 [64, 4], P(('parts', 'pair')), may hold values from 0 to 5, as said below
- aggregate_low: int32 [8192], P(('parts', 'pair')), may hold values from 0 to 63
- coarse_ops: float32 [32, 5, 128, 128], P(('parts', 'pair')), as said below
- coarse_maps: int32 [32, 4, 128], P(('parts', 'pair')), may hold values from 0 to 63, as said below
Outputs:
- solution: float32 [32, 65536], P(None, ('parts', 'pair'))
The draws below stay inside these ranges and needn't reach their ends.
Inputs may be any that keep to these rules, and one draw needn't show every extreme that they name: `columns_fine`: row tile i of a device's tiles lists positions of its extended vector: entry 0 is i + 2, the others lie in i to i + 4; the first 2 row tiles reach the tiles before and the last 2 the tiles after. `columns_mid`: as for columns_fine, with 4 tiles a device. `columns_low`: as for columns_fine, with 2 tiles a device. `coarse_ops`: entry [d, j] is equal on all devices d with the same d divided by 2^(j+1), rounded down. `coarse_maps`: entry [d, j] is equal on all devices d with the same d divided by 2^(j+1), rounded down.
All inputs are finite; a program needn't handle non-finite values.
Results may differ from the reference program's by a relative error of at most 0.0003.
Values sent between devices are 32-bit elements; how exact they have to be, the bound alone decides.
No kernel may reach another device: no remote copies, remote signals or barrier semaphores. Data moves between devices by JAX's collectives and lax.ppermute only.
A program may use at most 128 MiB of HBM per device.

```python
import math
import jax
import jax.numpy as jnp
from jax import lax

NRHS = 32
TILE = 128
PIECE = 64
LINKS = 4
HALO = 2
TILES0 = 16
TILES1 = 4
TILES2 = 2
LEVELS = 5
SWEEPS = 3
COARSE_SWEEPS = 2
COARSEST_SWEEPS = 8
ROWS0 = 65536
ROWS1 = 16384
ROWS2 = 8192
DEVICES = 32


def draw_tile_blocks(key, total_tiles, level_scale, entry_low, entry_high, attach_low, attach_high):
    first, second = jax.random.split(key)
    entries = -level_scale / (LINKS * TILE) * jax.random.uniform(first, (total_tiles, LINKS, TILE, TILE), jnp.float32, entry_low, entry_high)
    attach = jnp.exp(jax.random.uniform(second, (total_tiles, TILE), jnp.float32, math.log(attach_low), math.log(attach_high)))
    identity = jnp.eye(TILE, dtype=jnp.float32)
    return entries.at[:, 0].add((level_scale * (1.0 + attach))[:, :, None] * identity)


def tile_columns(key, total_tiles, tile_count):
    local_tile = jnp.arange(total_tiles, dtype=jnp.int32) % tile_count
    offsets = jax.random.randint(key, (total_tiles, LINKS - 1), 0, 2 * HALO + 1, dtype=jnp.int32)
    others = local_tile[:, None] + offsets
    left_most = jnp.where(local_tile < HALO, local_tile, others[:, 0])
    right_most = jnp.where(local_tile >= tile_count - HALO, local_tile + 2 * HALO, others[:, 1])
    return jnp.concatenate([(local_tile + HALO)[:, None], left_most[:, None], right_most[:, None], others[:, 2:]], axis=1).astype(jnp.int32)


def spread_to_members(group_draws):
    depth_count = group_draws.shape[0]
    member = jnp.arange(DEVICES, dtype=jnp.int32)[:, None]
    group_index = member // (2 ** (jnp.arange(depth_count, dtype=jnp.int32) + 1))[None, :]
    return group_draws[jnp.arange(depth_count, dtype=jnp.int32)[None, :], group_index]


def group_matrices(key, entry_low, entry_high, attach_low, attach_high):
    first, second = jax.random.split(key)
    section_scale = TILES0 * jnp.exp2(jnp.arange(LEVELS, dtype=jnp.float32))
    entries = (-(section_scale / TILE))[:, None, None, None] * jax.random.uniform(first, (LEVELS, DEVICES, TILE, TILE), jnp.float32, entry_low, entry_high)
    attach = jnp.exp(jax.random.uniform(second, (LEVELS, DEVICES, TILE), jnp.float32, math.log(attach_low), math.log(attach_high)))
    identity = jnp.eye(TILE, dtype=jnp.float32)
    return spread_to_members(entries + (section_scale[:, None, None] * (1.0 + attach))[:, :, :, None] * identity)


def draw_pulse_rhs(key, part):
    key = jax.random.fold_in(key, 9)
    return jax.random.truncated_normal(key, -6.0, 6.0, (NRHS, ROWS0), jnp.float32)


def draw_blocks_fine(key, part):
    key = jax.random.fold_in(key, 1)
    return draw_tile_blocks(key, TILES0 * DEVICES, 1.0, 0.5, 1.5, 0.05, 0.5)


def draw_blocks_mid(key, part):
    key = jax.random.fold_in(key, 2)
    return draw_tile_blocks(key, TILES1 * DEVICES, 1.0 * (TILES0 // TILES1), 0.5, 1.5, 0.05, 0.5)


def draw_blocks_low(key, part):
    key = jax.random.fold_in(key, 3)
    return draw_tile_blocks(key, TILES2 * DEVICES, 1.0 * (TILES0 // TILES2), 0.5, 1.5, 0.05, 0.5)


def draw_columns_fine(key, part):
    key = jax.random.fold_in(key, 4)
    return tile_columns(key, TILES0 * DEVICES, TILES0)


def draw_columns_mid(key, part):
    key = jax.random.fold_in(key, 5)
    return tile_columns(key, TILES1 * DEVICES, TILES1)


def draw_columns_low(key, part):
    key = jax.random.fold_in(key, 6)
    return tile_columns(key, TILES2 * DEVICES, TILES2)


def draw_coarse_ops(key, part):
    key = jax.random.fold_in(key, 7)
    return group_matrices(key, 0.5, 1.5, 0.05, 0.5)


def draw_coarse_maps(key, part):
    key = jax.random.fold_in(key, 8)
    group_draws = jax.random.randint(key, (LEVELS - 1, DEVICES, TILE), 0, PIECE, dtype=jnp.int32)
    return spread_to_members(group_draws).astype(jnp.int32)


def place_ends(drawn, own_key, least, high):
    place = [jax.random.randint(jax.random.fold_in(own_key, axis), (), 0, length) for axis, length in enumerate(drawn.shape)]
    main_axis = drawn.shape.index(max(drawn.shape))
    next_to = place[:main_axis] + [(place[main_axis] + 1) % drawn.shape[main_axis]] + place[main_axis + 1:]
    return drawn.at[tuple(place)].set(least).at[tuple(next_to)].set(high)


def setup_inputs(seed: int = 0) -> dict:
    key_of = jax.random.split(jax.random.key(seed), 13)
    pulse_rhs = draw_pulse_rhs(jax.random.fold_in(key_of[12], 71), 0)
    blocks_fine = draw_blocks_fine(jax.random.fold_in(key_of[12], 71), 0)
    columns_fine = draw_columns_fine(jax.random.fold_in(key_of[12], 71), 0)
    aggregate_fine = place_ends(jax.random.randint(key_of[3], (ROWS0,), 0, TILE), jax.random.fold_in(key_of[3], 1), 0, TILE - 1).astype(jnp.int32)
    blocks_mid = draw_blocks_mid(jax.random.fold_in(key_of[12], 71), 0)
    columns_mid = draw_columns_mid(jax.random.fold_in(key_of[12], 71), 0)
    aggregate_mid = place_ends(jax.random.randint(key_of[6], (ROWS1,), 0, TILE), jax.random.fold_in(key_of[6], 1), 0, TILE - 1).astype(jnp.int32)
    blocks_low = draw_blocks_low(jax.random.fold_in(key_of[12], 71), 0)
    columns_low = draw_columns_low(jax.random.fold_in(key_of[12], 71), 0)
    aggregate_low = place_ends(jax.random.randint(key_of[9], (ROWS2,), 0, PIECE), jax.random.fold_in(key_of[9], 1), 0, PIECE - 1).astype(jnp.int32)
    coarse_ops = draw_coarse_ops(jax.random.fold_in(key_of[12], 71), 0)
    coarse_maps = draw_coarse_maps(jax.random.fold_in(key_of[12], 71), 0)
    return dict(pulse_rhs=pulse_rhs, blocks_fine=blocks_fine, columns_fine=columns_fine, aggregate_fine=aggregate_fine, blocks_mid=blocks_mid, columns_mid=columns_mid, aggregate_mid=aggregate_mid, blocks_low=blocks_low, columns_low=columns_low, aggregate_low=aggregate_low, coarse_ops=coarse_ops, coarse_maps=coarse_maps)


OMEGA = 0.7


def tile_product(blocks, columns, extended):
    picked = extended[:, columns]
    return jnp.einsum("tkrc,btkc->btr", blocks, picked, precision=lax.Precision.HIGHEST)


def level_apply(blocks, columns, vector, tile_count):
    total_tiles = vector.shape[1]
    padded = jnp.pad(vector, ((0, 0), (HALO, HALO), (0, 0)))

    def one_device(device):
        first_tile = (device * tile_count).astype(jnp.int32)
        extended = lax.dynamic_slice_in_dim(padded, first_tile, tile_count + 2 * HALO, 1)
        local_blocks = lax.dynamic_slice_in_dim(blocks, first_tile, tile_count, 0)
        local_columns = lax.dynamic_slice_in_dim(columns, first_tile, tile_count, 0)
        return tile_product(local_blocks, local_columns, extended)

    result = lax.map(one_device, jnp.arange(total_tiles // tile_count, dtype=jnp.int32))
    return jnp.transpose(result, (1, 0, 2, 3)).reshape(vector.shape)


def level_diagonal(blocks, columns, tile_count):
    own_tile = (jnp.arange(blocks.shape[0], dtype=jnp.int32) % tile_count) + HALO
    own_hits = (columns == own_tile[:, None]).astype(jnp.float32)
    return jnp.sum(jnp.diagonal(blocks, axis1=2, axis2=3) * own_hits[:, :, None], axis=1)


def smooth_fine(blocks, columns, tile_count, diagonal, source, iterate, sweeps):
    for sweep_index in range(sweeps):
        iterate = iterate + OMEGA * (source - level_apply(blocks, columns, iterate, tile_count)) / diagonal
    return iterate


def coarse_apply(matrices, vector):
    return jnp.einsum("gij,bgj->bgi", matrices, vector, precision=lax.Precision.HIGHEST)


def smooth_coarse(matrices, diagonal, source, iterate, sweeps):
    for sweep_index in range(sweeps):
        iterate = iterate + OMEGA * (source - coarse_apply(matrices, iterate)) / diagonal
    return iterate


def coarse_chain(pieces, coarse_ops, coarse_maps):
    stored = []
    for section_index in range(LEVELS):
        group_span = 2 ** (section_index + 1)
        groups = DEVICES // group_span
        merged = pieces.reshape(NRHS, groups, TILE)
        leaders = jnp.arange(groups, dtype=jnp.int32) * group_span
        matrices = coarse_ops[leaders, section_index]
        diagonal = jnp.diagonal(matrices, axis1=1, axis2=2)
        sweeps = COARSEST_SWEEPS if section_index == LEVELS - 1 else COARSE_SWEEPS
        iterate = smooth_coarse(matrices, diagonal, merged, OMEGA * merged / diagonal, sweeps - 1)
        segment = None
        if section_index < LEVELS - 1:
            residual = (merged - coarse_apply(matrices, iterate)).reshape(NRHS, groups * TILE)
            segment = (jnp.arange(groups, dtype=jnp.int32)[:, None] * PIECE + coarse_maps[leaders, section_index]).reshape(-1)
            pieces = jax.ops.segment_sum(residual.T, segment, num_segments=groups * PIECE).T
        stored.append((merged, iterate, matrices, diagonal, segment))
    halves = None
    for section_index in reversed(range(LEVELS)):
        merged, iterate, matrices, diagonal, segment = stored[section_index]
        if section_index < LEVELS - 1:
            iterate = iterate + halves[:, segment].reshape(iterate.shape)
            iterate = smooth_coarse(matrices, diagonal, merged, iterate, COARSE_SWEEPS)
        halves = iterate.reshape(NRHS, -1)
    return halves


def fine_cycle(levels, counts, level_index, source, coarse_ops, coarse_maps):
    blocks, columns, aggregate = levels[level_index]
    tile_count = counts[level_index]
    diagonal = level_diagonal(blocks, columns, tile_count)
    iterate = smooth_fine(blocks, columns, tile_count, diagonal, source, OMEGA * source / diagonal, SWEEPS - 1)
    residual = (source - level_apply(blocks, columns, iterate, tile_count)).reshape(NRHS, -1)
    row_ids = jnp.arange(aggregate.shape[0], dtype=jnp.int32)
    if level_index < 2:
        factor = tile_count // counts[level_index + 1]
        segment = ((row_ids // TILE) // factor) * TILE + aggregate
        coarse_rows = residual.shape[1] // factor
    else:
        segment = (row_ids // (tile_count * TILE)) * PIECE + aggregate
        coarse_rows = DEVICES * PIECE
    coarse_source = jax.ops.segment_sum(residual.T, segment, num_segments=coarse_rows).T
    if level_index < 2:
        correction = fine_cycle(levels, counts, level_index + 1, coarse_source.reshape(NRHS, -1, TILE), coarse_ops, coarse_maps).reshape(NRHS, -1)
    else:
        correction = coarse_chain(coarse_source, coarse_ops, coarse_maps)
    iterate = iterate + correction[:, segment].reshape(iterate.shape)
    return smooth_fine(blocks, columns, tile_count, diagonal, source, iterate, SWEEPS)


def reference(pulse_rhs, blocks_fine, columns_fine, aggregate_fine, blocks_mid, columns_mid, aggregate_mid, blocks_low, columns_low, aggregate_low, coarse_ops, coarse_maps):
    levels = ((blocks_fine, columns_fine, aggregate_fine), (blocks_mid, columns_mid, aggregate_mid), (blocks_low, columns_low, aggregate_low))
    counts = (TILES0, TILES1, TILES2)
    source = pulse_rhs.reshape(NRHS, TILES0 * DEVICES, TILE)
    result = fine_cycle(levels, counts, 0, source, coarse_ops, coarse_maps)
    return result.reshape(NRHS, ROWS0)
```

```python
import functools

import jax
import jax.numpy as jnp
from jax import lax
from jax.experimental import pallas as pl
from jax.experimental.pallas import tpu as pltpu
from jax.sharding import PartitionSpec as P

HALO = 2
COARSE_SWEEPS = 2
COARSEST_SWEEPS = 8
OMEGA = 0.7
AXES = ("parts", "pair")
NT = (((1,), (1,)), ((), ()))
NN = (((1,), (0,)), ((), ()))
F32 = jnp.float32
BF16 = jnp.bfloat16


def split(value):
    high = value.astype(BF16)
    return high, (value - high.astype(F32)).astype(BF16)


def stack(value):
    return jnp.concatenate(split(value), axis=0)


def fold_rows(value):
    half = value.shape[0] // 2
    return value[:half] + value[half:]


def product(stacked, weights, dims, width):
    full = lax.dot_general(stacked, weights, dims, preferred_element_type=F32)
    rows = full.shape[0] // 2
    return full[:rows, :width] + (full[:rows, width:] + full[rows:, :width])


def picked_sum(stacked, one_hot, dims):
    return fold_rows(lax.dot_general(stacked, one_hot, dims, preferred_element_type=F32))


def position():
    return lax.axis_index("parts") * lax.axis_size("pair") + lax.axis_index("pair")


def diagonal_row(block):
    size = block.shape[-1]
    rows = lax.broadcasted_iota(jnp.int32, (size, size), 0)
    lanes = lax.broadcasted_iota(jnp.int32, (size, size), 1)
    return jnp.sum(jnp.where(rows == lanes, block, 0.0), axis=0, keepdims=True)


def tile_diagonal(columns, blocks, tile):
    total = None
    for link in range(blocks.shape[1]):
        own = (columns[tile, link] == tile + HALO).astype(F32)
        term = diagonal_row(blocks[tile, link]) * own
        total = term if total is None else total + term
    return total


def get_tile(ref, tile, panels, width):
    if ref.shape[0] == panels:
        return ref[:, tile * width:(tile + 1) * width]
    return ref[pl.ds(tile * panels, panels)]


def put_tile(ref, tile, value, panels, width):
    if ref.shape[0] == panels and ref.shape[1] != width:
        ref[:, tile * width:(tile + 1) * width] = value
    else:
        ref[pl.ds(tile * panels, panels)] = value


def fill_extended(extended, vector, pair_halo, chip_halo, count, panels):
    core = lax.axis_index("pair")
    for tile in range(count):
        extended[tile + HALO] = stack(vector[pl.ds(tile * panels, panels)])
    for tile in range(HALO):
        rows = pl.ds(tile * panels, panels)
        extended[core * (count + HALO) + tile] = stack(chip_halo[rows])
        extended[(1 - core) * (count + HALO) + tile] = stack(pair_halo[rows])


def tile_apply(columns, blocks, extended, tile):
    links, width = blocks.shape[1], blocks.shape[-1]
    left = jnp.concatenate([extended[columns[tile, k]] for k in range(links)], axis=1)
    parts = [split(blocks[tile, k]) for k in range(links)]
    weights = jnp.concatenate(
        [jnp.concatenate([p[0] for p in parts], axis=1), jnp.concatenate([p[1] for p in parts], axis=1)], axis=0
    )
    return product(left, weights, NT, width)


def put_edges(vector, count, panels, pair_edge, chip_edge):
    core = lax.axis_index("pair")
    last = (count - HALO) * panels
    size = HALO * panels
    pair_edge[...] = vector[pl.ds(pl.multiple_of((1 - core) * last, panels), size)]
    chip_edge[...] = vector[pl.ds(pl.multiple_of(core * last, panels), size)]


def first_kernel(columns, source, blocks, diagonal, vector, pair_edge, chip_edge):
    panels = source.shape[0]
    count, width = blocks.shape[0], blocks.shape[-1]
    for tile in range(count):
        row = tile_diagonal(columns, blocks, tile)
        diagonal[pl.ds(tile, 1)] = row
        vector[pl.ds(tile * panels, panels)] = OMEGA * get_tile(source, tile, panels, width) / row
    put_edges(vector, count, panels, pair_edge, chip_edge)


def sweep_kernel(panels, edges, columns, vector, pair_halo, chip_halo, source, diagonal, blocks, result, *rest):
    extended = rest[-1]
    count, width = blocks.shape[0], blocks.shape[-1]
    fill_extended(extended, vector, pair_halo, chip_halo, count, panels)
    for tile in range(count):
        product_tile = tile_apply(columns, blocks, extended, tile)
        old = vector[pl.ds(tile * panels, panels)]
        new = old + OMEGA * (get_tile(source, tile, panels, width) - product_tile) / diagonal[pl.ds(tile, 1)]
        put_tile(result, tile, new, panels, width)
    if edges:
        put_edges(result, count, panels, rest[0], rest[1])


def residual_kernel(
    panels, columns, vector, pair_halo, chip_halo, source, blocks, aggregate, next_columns, next_blocks,
    next_source, next_diagonal, next_vector, pair_edge, chip_edge, extended,
):
    count, width = blocks.shape[0], blocks.shape[-1]
    next_count = next_blocks.shape[0]
    factor = count // next_count
    fill_extended(extended, vector, pair_halo, chip_halo, count, panels)
    for group in range(next_count):
        pieces = []
        for tile in range(group * factor, (group + 1) * factor):
            rest = get_tile(source, tile, panels, width) - tile_apply(columns, blocks, extended, tile)
            pieces.append(stack(rest))
        one_hot = one_hot_rows(aggregate[:, group * factor * width:(group + 1) * factor * width], width)
        gathered = picked_sum(jnp.concatenate(pieces, axis=1), one_hot, NT)
        row = tile_diagonal(next_columns, next_blocks, group)
        rows = pl.ds(group * panels, panels)
        next_source[rows] = gathered
        next_diagonal[pl.ds(group, 1)] = row
        next_vector[rows] = OMEGA * gathered / row
    put_edges(next_vector, next_count, panels, pair_edge, chip_edge)


def one_hot_rows(indices, width):
    rows = lax.broadcasted_iota(jnp.int32, (width, indices.shape[1]), 0)
    return (rows == indices).astype(F32).astype(BF16)


def one_hot_twice(indices, width):
    rows = lax.broadcasted_iota(jnp.int32, (width, indices.shape[1]), 0)
    half = width // 2
    return (jnp.where(rows < half, rows, rows - half) == indices).astype(F32).astype(BF16)


def prolong_kernel(
    panels, columns, vector, pair_halo, chip_halo, source, diagonal, blocks, aggregate, upper,
    next_vector, pair_edge, chip_edge, extended,
):
    count, width = blocks.shape[0], blocks.shape[-1]
    upper_count = upper.shape[0] // panels
    factor = upper_count // count
    fill_extended(extended, vector, pair_halo, chip_halo, count, panels)
    for tile in range(count):
        product_tile = tile_apply(columns, blocks, extended, tile)
        old = vector[pl.ds(tile * panels, panels)]
        new = old + OMEGA * (get_tile(source, tile, panels, width) - product_tile) / diagonal[pl.ds(tile, 1)]
        one_hot = one_hot_rows(aggregate[:, tile * factor * width:(tile + 1) * factor * width], width)
        lifted = picked_sum(stack(new), one_hot, NN)
        for k in range(factor):
            rows = pl.ds((tile * factor + k) * panels, panels)
            next_vector[rows] = upper[rows] + lifted[:, k * width:(k + 1) * width]
    put_edges(next_vector, upper_count, panels, pair_edge, chip_edge)


def chain_weights(operators, depths):
    weights, diagonals = [], []
    for level in range(depths):
        matrix = operators[0, level]
        weights.append(jnp.concatenate(split(matrix), axis=0))
        diagonals.append(diagonal_row(matrix))
    return weights, diagonals


def coarse_apply(weights, value):
    return product(stack(value), weights, NT, value.shape[1])


def coarse_sweeps(weights, diagonal, source, value, sweeps):
    for _ in range(sweeps):
        value = value + OMEGA * (source - coarse_apply(weights, value)) / diagonal
    return value


def lane_half(rows, width):
    return (lax.broadcasted_iota(jnp.int32, (rows, width), 1) >= width // 2).astype(jnp.int32)


def maps_kernel(operators, maps, result):
    depths, width = operators.shape[1], operators.shape[-1]
    half = width // 2
    here = position()
    weights, diagonals = chain_weights(operators, depths - 1)
    lanes = lax.broadcasted_iota(jnp.int32, (half, width), 1)
    rows = lax.broadcasted_iota(jnp.int32, (half, width), 0)
    piece = (jnp.where(lanes < half, lanes, lanes - half) == rows).astype(F32)
    halves = lane_half(half, width)
    for level in range(depths):
        high, low = split(piece)
        result[:, 2 * level * width:(2 * level + 1) * width] = high
        result[:, (2 * level + 1) * width:(2 * level + 2) * width] = low
        if level < depths - 1:
            bit = (here >> level) & 1
            merged = jnp.where(halves == bit, piece, 0.0)
            value = coarse_sweeps(
                weights[level], diagonals[level], merged, OMEGA * merged / diagonals[level], COARSE_SWEEPS - 1
            )
            rest = merged - coarse_apply(weights[level], value)
            piece = picked_sum(stack(rest), one_hot_twice(maps[0, pl.ds(level, 1)], width), NT)


def lowest_kernel(
    panels, columns, vector, pair_halo, chip_halo, source, blocks, aggregate, images,
    own_piece, outgoing, extended,
):
    count, width = blocks.shape[0], blocks.shape[-1]
    half = width // 2
    here = position()
    fill_extended(extended, vector, pair_halo, chip_halo, count, panels)
    pieces = []
    for tile in range(count):
        rest = get_tile(source, tile, panels, width) - tile_apply(columns, blocks, extended, tile)
        pieces.append(stack(rest))
    one_hot = one_hot_twice(aggregate[...], width)
    gathered = picked_sum(jnp.concatenate(pieces, axis=1), one_hot, NT)
    own_piece[...] = gathered
    shares = lax.dot_general(stack(gathered)[:, :half], images[...], NN, preferred_element_type=F32)
    depths = images.shape[1] // (2 * width)
    top = lax.broadcasted_iota(jnp.int32, (panels // 2, width), 1) < half
    for level in range(depths):
        low = shares[:, 2 * level * width:(2 * level + 2) * width]
        share = low[:panels, :width] + (low[:panels, width:] + low[panels:, :width])
        packed = jnp.where(top, share[:panels // 2], share[panels // 2:])
        start = ((here >> level) ^ 1) << level
        if level == 0:
            outgoing[pl.ds(here, 1)] = packed[None]
        outgoing[pl.ds(start, 2**level)] = jnp.broadcast_to(packed[None], (2**level,) + packed.shape)


def chain_kernel(panels, own_piece, incoming, operators, maps, aggregate, upper, result):
    depths, width = operators.shape[1], operators.shape[-1]
    half = width // 2
    here = position()
    weights, diagonals = chain_weights(operators, depths)
    halves = lane_half(panels, width)
    top = lax.broadcasted_iota(jnp.int32, (panels // 2, width), 1) < half
    piece = own_piece[...]
    stored = []
    for level in range(depths):
        bit = (here >> level) & 1
        start = ((here >> level) ^ 1) << level
        packed = jnp.sum(incoming[pl.ds(start, 2**level)], axis=0)
        swapped = jnp.concatenate([packed[:, half:], packed[:, :half]], axis=1)
        other = jnp.concatenate([jnp.where(top, packed, swapped), jnp.where(top, swapped, packed)], axis=0)
        merged = jnp.where(halves == bit, piece, other)
        sweeps = COARSEST_SWEEPS if level == depths - 1 else COARSE_SWEEPS
        value = coarse_sweeps(weights[level], diagonals[level], merged, OMEGA * merged / diagonals[level], sweeps - 1)
        stored.append((merged, value))
        if level < depths - 1:
            rest = merged - coarse_apply(weights[level], value)
            piece = picked_sum(stack(rest), one_hot_twice(maps[0, pl.ds(level, 1)], width), NT)
    for level in reversed(range(depths)):
        merged, below = stored[level]
        if level < depths - 1:
            bit = (here >> (level + 1)) & 1
            one_hot = one_hot_rows(maps[0, pl.ds(level, 1)] + bit * half, width)
            value = below + picked_sum(stack(value), one_hot, NN)
            value = coarse_sweeps(weights[level], diagonals[level], merged, value, COARSE_SWEEPS)
    one_hot = one_hot_rows(aggregate[...] + (here & 1) * half, width)
    lifted = picked_sum(stack(value), one_hot, NN)
    for tile in range(aggregate.shape[1] // width):
        rows = pl.ds(tile * panels, panels)
        result[rows] = upper[rows] + lifted[:, tile * width:(tile + 1) * width]


def call(kernel, shapes, operands, scalars=(), scratch=(), name=None):
    vmem = pl.BlockSpec(memory_space=pltpu.VMEM)
    smem = pl.BlockSpec(memory_space=pltpu.SMEM)
    specs = [smem if k in scalars else vmem for k in range(len(operands))]
    outs = pl.pallas_call(
        kernel,
        out_shape=[jax.ShapeDtypeStruct(s, t) for s, t in shapes],
        in_specs=specs,
        out_specs=[vmem] * len(shapes),
        scratch_shapes=list(scratch),
        compiler_params=pltpu.CompilerParams(vmem_limit_bytes=32 * 2**20),
        name=name,
    )(*operands)
    return outs


def swaps(pairs):
    return [p for a, b in pairs for p in ((a, b), (b, a))]


def exchange(pair_edge, chip_edge):
    count = lax.axis_size(AXES)
    inner = swaps([(2 * k, 2 * k + 1) for k in range(count // 2)])
    outer = swaps([(2 * k + 1, 2 * k + 2) for k in range(count // 2 - 1)])
    return lax.ppermute(pair_edge, AXES, inner), lax.ppermute(chip_edge, AXES, outer)


def on_device(
    pulse_rhs, blocks_fine, columns_fine, aggregate_fine, blocks_mid, columns_mid, aggregate_mid,
    blocks_low, columns_low, aggregate_low, coarse_ops, coarse_maps,
):
    panels, width = pulse_rhs.shape[0], blocks_fine.shape[-1]
    devices = lax.axis_size(AXES)
    blocks = (blocks_fine, blocks_mid, blocks_low)
    columns = (columns_fine, columns_mid, columns_low)
    aggregates = tuple(a.reshape(1, -1) for a in (aggregate_fine, aggregate_mid, aggregate_low))
    counts = tuple(b.shape[0] for b in blocks)
    depths = coarse_ops.shape[1]

    def vec(level):
        return ((counts[level] * panels, width), F32)

    def diag(level):
        return ((counts[level], width), F32)

    edge = ((HALO * panels, width), F32)

    def ext(level):
        return [pltpu.VMEM((counts[level] + 2 * HALO, 2 * panels, width), BF16)]

    def sweep(level, vector, halos, last=False):
        shapes = [(pulse_rhs.shape, F32)] if last else [vec(level), edge, edge]
        outs = call(
            functools.partial(sweep_kernel, panels, not last),
            shapes,
            (columns[level], vector, *halos, sources[level], diagonals[level], blocks[level]),
            scalars=(0,), scratch=ext(level), name=f"sweep{level}",
        )
        return outs[0] if last else (outs[0], exchange(outs[1], outs[2]))

    images = call(maps_kernel, [((width // 2, 2 * depths * width), BF16)], (coarse_ops, coarse_maps), name="maps")[0]
    sources, diagonals, kept = [pulse_rhs], [], []
    diagonal, vector, pair_edge, chip_edge = call(
        first_kernel, [diag(0), vec(0), edge, edge], (columns[0], pulse_rhs, blocks[0]), scalars=(0,), name="first"
    )
    diagonals.append(diagonal)
    halos = exchange(pair_edge, chip_edge)
    for level in range(3):
        vector, halos = sweep(level, vector, halos)
        vector, halos = sweep(level, vector, halos)
        kept.append(vector)
        if level < 2:
            source, diagonal, vector, pair_edge, chip_edge = call(
                functools.partial(residual_kernel, panels),
                [vec(level + 1), diag(level + 1), vec(level + 1), edge, edge],
                (columns[level], vector, *halos, sources[level], blocks[level], aggregates[level],
                 columns[level + 1], blocks[level + 1]),
                scalars=(0, 7), scratch=ext(level), name=f"residual{level}",
            )
            sources.append(source)
            diagonals.append(diagonal)
            halos = exchange(pair_edge, chip_edge)
    own_piece, outgoing = call(
        functools.partial(lowest_kernel, panels),
        [((panels, width), F32), ((devices, panels // 2, width), F32)],
        (columns[2], vector, *halos, sources[2], blocks[2], aggregates[2], images),
        scalars=(0,), scratch=ext(2), name="lowest",
    )
    incoming = lax.all_to_all(outgoing, AXES, 0, 0)
    vector = call(
        functools.partial(chain_kernel, panels), [vec(2)],
        (own_piece, incoming, coarse_ops, coarse_maps, aggregates[2], kept[2]), name="chain",
    )[0]
    halos = exchange(vector, vector)
    for level in (2, 1, 0):
        vector, halos = sweep(level, vector, halos)
        vector, halos = sweep(level, vector, halos)
        if level == 0:
            return sweep(0, vector, halos, last=True)
        vector, pair_edge, chip_edge = call(
            functools.partial(prolong_kernel, panels), [vec(level - 1), edge, edge],
            (columns[level], vector, *halos, sources[level], diagonals[level], blocks[level],
             aggregates[level - 1], kept[level - 1]),
            scalars=(0,), scratch=ext(level), name=f"prolong{level}",
        )
        halos = exchange(pair_edge, chip_edge)


def solution(mesh):
    split_first = P(AXES)
    rhs = P(None, AXES)
    return jax.shard_map(
        on_device, mesh=mesh, in_specs=(rhs,) + (split_first,) * 11, out_specs=rhs, check_vma=False
    )
```

```python
import functools

import jax
import jax.numpy as jnp
from jax import lax
from jax.experimental import pallas as pl
from jax.experimental.pallas import tpu as pltpu
from jax.sharding import PartitionSpec as P

HALO = 2
VMEM_BYTES = 24 * 2**20
COARSE_SWEEPS = 2
COARSEST_SWEEPS = 8
OMEGA = 0.7
AXES = ("parts", "pair")
NT = (((1,), (1,)), ((), ()))
NN = (((1,), (0,)), ((), ()))
F32 = jnp.float32
BF16 = jnp.bfloat16


def split(value):
    high = value.astype(BF16)
    return high, (value - high.astype(F32)).astype(BF16)


def stack(value):
    return jnp.concatenate(split(value), axis=0)


def fold_rows(value):
    half = value.shape[0] // 2
    return value[:half] + value[half:]


def product(stacked, weights, dims, width):
    full = lax.dot_general(stacked, weights, dims, preferred_element_type=F32)
    rows = full.shape[0] // 2
    return full[:rows, :width] + (full[:rows, width:] + full[rows:, :width])


def picked_sum(stacked, one_hot, dims):
    return fold_rows(lax.dot_general(stacked, one_hot, dims, preferred_element_type=F32))


def position():
    return lax.axis_index("parts") * lax.axis_size("pair") + lax.axis_index("pair")


def diagonal_row(block):
    size = block.shape[-1]
    rows = lax.broadcasted_iota(jnp.int32, (size, size), 0)
    lanes = lax.broadcasted_iota(jnp.int32, (size, size), 1)
    return jnp.sum(jnp.where(rows == lanes, block, 0.0), axis=0, keepdims=True)


def column(columns, blocks, tile, link):
    if columns.shape == blocks.shape[:2]:
        return columns[tile, link]
    return columns[link, tile]


def tile_diagonal(columns, blocks, tile):
    total = None
    for link in range(blocks.shape[1]):
        own = (column(columns, blocks, tile, link) == tile + HALO).astype(F32)
        term = diagonal_row(blocks[tile, link]) * own
        total = term if total is None else total + term
    return total


def get_tile(ref, tile, panels, width):
    if ref.shape[0] == panels:
        return ref[:, tile * width:(tile + 1) * width]
    return ref[pl.ds(tile * panels, panels)]


def put_tile(ref, tile, value, panels, width):
    if ref.shape[0] == panels and ref.shape[1] != width:
        ref[:, tile * width:(tile + 1) * width] = value
    else:
        ref[pl.ds(tile * panels, panels)] = value


def fill_extended(extended, vector, pair_halo, chip_halo, count, panels):
    core = lax.axis_index("pair")
    for tile in range(count):
        extended[tile + HALO] = stack(vector[pl.ds(tile * panels, panels)])
    for tile in range(HALO):
        rows = pl.ds(tile * panels, panels)
        extended[core * (count + HALO) + tile] = stack(chip_halo[rows])
        extended[(1 - core) * (count + HALO) + tile] = stack(pair_halo[rows])


def weights_of(blocks, tile):
    parts = [split(blocks[tile, k]) for k in range(blocks.shape[1])]
    return jnp.concatenate(
        [jnp.concatenate([p[0] for p in parts], axis=1), jnp.concatenate([p[1] for p in parts], axis=1)], axis=0
    )


def tile_apply(columns, blocks, extended, tile, shift=0):
    picked = [extended[column(columns, blocks, tile, k) + shift] for k in range(blocks.shape[1])]
    return product(jnp.concatenate(picked, axis=1), weights_of(blocks, tile), NT, blocks.shape[-1])


def put_edges(vector, count, panels, pair_edge, chip_edge):
    core = lax.axis_index("pair")
    last = (count - HALO) * panels
    size = HALO * panels
    pair_edge[pl.ds(0, size)] = vector[pl.ds(pl.multiple_of((1 - core) * last, panels), size)]
    chip_edge[pl.ds(0, size)] = vector[pl.ds(pl.multiple_of(core * last, panels), size)]


def put_wide_edges(vector, count, panels, wide, pair_edge, chip_edge):
    core = lax.axis_index("pair")
    reach = wide - HALO
    for edge, turn in ((pair_edge, 1 - core), (chip_edge, core)):
        near = pl.multiple_of(turn * (count - reach) * panels, panels)
        far = pl.multiple_of(jnp.where(turn == 1, count - wide, reach) * panels, panels)
        edge[pl.ds(0, reach * panels)] = vector[pl.ds(near, reach * panels)]
        edge[pl.ds(reach * panels, HALO * panels)] = vector[pl.ds(far, HALO * panels)]


def integer_row(values, width):
    lanes = lax.broadcasted_iota(jnp.int32, (8, width), 1)
    row = jnp.zeros((8, width), F32)
    for k, value in enumerate(values):
        row = jnp.where(lanes == k, value.astype(F32), row)
    return row


def columns_row(columns, blocks, first, tiles, width):
    links = blocks.shape[1]
    return integer_row([column(columns, blocks, first + t, k) for t in range(tiles) for k in range(links)], width)


def first_kernel(reach, columns, source, blocks, diagonal, vector, pair_edge, chip_edge):
    panels = source.shape[0]
    count, width = blocks.shape[0], blocks.shape[-1]
    core = lax.axis_index("pair")
    start = HALO * panels
    for edge, turn in ((pair_edge, 1 - core), (chip_edge, core)):
        edge[pl.ds(start, 8)] = columns_row(columns, blocks, turn * (count - reach), reach, width)
        for tile in range(reach):
            ahead, behind = get_tile(source, tile, panels, width), get_tile(source, count - reach + tile, panels, width)
            edge[pl.ds(start + 8 + tile * panels, panels)] = jnp.where(turn == 1, behind, ahead)
    for tile in range(count):
        row = tile_diagonal(columns, blocks, tile)
        diagonal[pl.ds(tile, 1)] = row
        vector[pl.ds(tile * panels, panels)] = OMEGA * get_tile(source, tile, panels, width) / row
    put_edges(vector, count, panels, pair_edge, chip_edge)


def copy_kernel(*_):
    pass


def sweep_kernel(panels, edges, columns, vector, pair_halo, chip_halo, source, diagonal, blocks, result, *rest):
    extended = rest[-1]
    count, width = blocks.shape[0], blocks.shape[-1]
    fill_extended(extended, vector, pair_halo, chip_halo, count, panels)
    for tile in range(count):
        product_tile = tile_apply(columns, blocks, extended, tile)
        old = vector[pl.ds(tile * panels, panels)]
        new = old + OMEGA * (get_tile(source, tile, panels, width) - product_tile) / diagonal[pl.ds(tile, 1)]
        put_tile(result, tile, new, panels, width)
    if edges:
        put_edges(result, count, panels, rest[0], rest[1])


def restrict(pieces, aggregate, next_columns, next_blocks, panels, next_source, next_diagonal, next_vector):
    width, next_count = next_blocks.shape[-1], next_blocks.shape[0]
    factor = len(pieces) // next_count
    for group in range(next_count):
        one_hot = one_hot_rows(aggregate[:, group * factor * width:(group + 1) * factor * width], width)
        stacked = jnp.concatenate([stack(p) for p in pieces[group * factor:(group + 1) * factor]], axis=1)
        gathered = picked_sum(stacked, one_hot, NT)
        row = tile_diagonal(next_columns, next_blocks, group)
        rows = pl.ds(group * panels, panels)
        next_source[rows] = gathered
        next_diagonal[pl.ds(group, 1)] = row
        next_vector[rows] = OMEGA * gathered / row


def residual_kernel(
    panels, columns, vector, pair_halo, chip_halo, source, blocks, aggregate, next_columns, next_blocks,
    next_source, next_diagonal, next_vector, packed, extended,
):
    count, width = blocks.shape[0], blocks.shape[-1]
    fill_extended(extended, vector, pair_halo, chip_halo, count, panels)
    pieces = [
        get_tile(source, tile, panels, width) - tile_apply(columns, blocks, extended, tile) for tile in range(count)
    ]
    restrict(pieces, aggregate, next_columns, next_blocks, panels, next_source, next_diagonal, next_vector)
    put_packed(packed, next_vector, panels, next_source, next_columns, next_blocks)


def put_packed(packed, vector, panels, source=None, columns=None, blocks=None):
    size, width = vector.shape
    packed[pl.ds(0, size)] = vector[...]
    at = size
    if source is not None:
        packed[pl.ds(at, size)] = source[...]
        packed[pl.ds(at + size, 8)] = columns_row(columns, blocks, 0, blocks.shape[0], width)
        at += size + 8
    if packed.shape[0] > at:
        edge = HALO * panels
        first = pl.multiple_of((1 - lax.axis_index("pair")) * (size - edge), panels)
        packed[pl.ds(at, edge)] = vector[pl.ds(first, edge)]


def one_hot_rows(indices, width):
    rows = lax.broadcasted_iota(jnp.int32, (width, indices.shape[1]), 0)
    return (rows == indices).astype(F32).astype(BF16)


def one_hot_twice(indices, width):
    rows = lax.broadcasted_iota(jnp.int32, (width, indices.shape[1]), 0)
    half = width // 2
    return (jnp.where(rows < half, rows, rows - half) == indices).astype(F32).astype(BF16)


def prolong(tile, value, aggregate, upper, panels, width, own_tiles, result):
    factor = upper.shape[0] // panels // own_tiles
    one_hot = one_hot_rows(aggregate[:, tile * factor * width:(tile + 1) * factor * width], width)
    lifted = picked_sum(stack(value), one_hot, NN)
    for k in range(factor):
        rows = pl.ds((tile * factor + k) * panels, panels)
        result[rows] = upper[rows] + lifted[:, k * width:(k + 1) * width]


def prolong_kernel(
    panels, columns, vector, pair_halo, chip_halo, source, diagonal, blocks, aggregate, upper,
    next_vector, packed, extended,
):
    count, width = blocks.shape[0], blocks.shape[-1]
    fill_extended(extended, vector, pair_halo, chip_halo, count, panels)
    for tile in range(count):
        product_tile = tile_apply(columns, blocks, extended, tile)
        old = vector[pl.ds(tile * panels, panels)]
        new = old + OMEGA * (get_tile(source, tile, panels, width) - product_tile) / diagonal[pl.ds(tile, 1)]
        prolong(tile, new, aggregate, upper, panels, width, count, next_vector)
    put_packed(packed, next_vector, panels)


def chain_weights(operators, depths):
    weights, diagonals = [], []
    for level in range(depths):
        matrix = operators[0, level]
        weights.append(jnp.concatenate(split(matrix), axis=0))
        diagonals.append(diagonal_row(matrix))
    return weights, diagonals


def coarse_apply(weights, value):
    return product(stack(value), weights, NT, value.shape[1])


def coarse_sweeps(weights, diagonal, source, value, sweeps):
    for _ in range(sweeps):
        value = value + OMEGA * (source - coarse_apply(weights, value)) / diagonal
    return value


def lane_half(rows, width):
    return (lax.broadcasted_iota(jnp.int32, (rows, width), 1) >= width // 2).astype(jnp.int32)


def maps_kernel(operators, maps, result):
    depths, width = operators.shape[1], operators.shape[-1]
    half = width // 2
    here = position()
    weights, diagonals = chain_weights(operators, depths - 1)
    lanes = lax.broadcasted_iota(jnp.int32, (half, width), 1)
    rows = lax.broadcasted_iota(jnp.int32, (half, width), 0)
    piece = (jnp.where(lanes < half, lanes, lanes - half) == rows).astype(F32)
    halves = lane_half(half, width)
    for level in range(depths):
        high, low = split(piece)
        result[:, 2 * level * width:(2 * level + 1) * width] = high
        result[:, (2 * level + 1) * width:(2 * level + 2) * width] = low
        if level < depths - 1:
            bit = (here >> level) & 1
            merged = jnp.where(halves == bit, piece, 0.0)
            value = coarse_sweeps(
                weights[level], diagonals[level], merged, OMEGA * merged / diagonals[level], COARSE_SWEEPS - 1
            )
            rest = merged - coarse_apply(weights[level], value)
            piece = picked_sum(stack(rest), one_hot_twice(maps[0, pl.ds(level, 1)], width), NT)


def send_shares(pieces, aggregate, images, panels, own_piece, outgoing):
    width = own_piece.shape[1]
    half = width // 2
    here = position()
    one_hot = one_hot_twice(aggregate[...], width)
    gathered = picked_sum(jnp.concatenate(pieces, axis=1), one_hot, NT)
    own_piece[...] = gathered
    shares = lax.dot_general(stack(gathered)[:, :half], images[...], NN, preferred_element_type=F32)
    depths = images.shape[1] // (2 * width)
    top = lax.broadcasted_iota(jnp.int32, (panels // 2, width), 1) < half
    for level in range(depths):
        low = shares[:, 2 * level * width:(2 * level + 2) * width]
        share = low[:panels, :width] + (low[:panels, width:] + low[panels:, :width])
        packed = jnp.where(top, share[:panels // 2], share[panels // 2:])
        start = ((here >> level) ^ 1) << level
        if level == 0:
            outgoing[pl.ds(here, 1)] = packed[None]
        outgoing[pl.ds(start, 2**level)] = jnp.broadcast_to(packed[None], (2**level,) + packed.shape)


def lowest_kernel(
    panels, columns, vector, pair_halo, chip_halo, source, blocks, aggregate, images,
    own_piece, outgoing, extended,
):
    count, width = blocks.shape[0], blocks.shape[-1]
    fill_extended(extended, vector, pair_halo, chip_halo, count, panels)
    pieces = []
    for tile in range(count):
        rest = get_tile(source, tile, panels, width) - tile_apply(columns, blocks, extended, tile)
        pieces.append(stack(rest))
    send_shares(pieces, aggregate, images, panels, own_piece, outgoing)


def chain_kernel(panels, own_piece, incoming, operators, maps, aggregate, upper, result):
    depths, width = operators.shape[1], operators.shape[-1]
    half = width // 2
    here = position()
    weights, diagonals = chain_weights(operators, depths)
    halves = lane_half(panels, width)
    top = lax.broadcasted_iota(jnp.int32, (panels // 2, width), 1) < half
    piece = own_piece[...]
    stored = []
    for level in range(depths):
        bit = (here >> level) & 1
        start = ((here >> level) ^ 1) << level
        packed = jnp.sum(incoming[pl.ds(start, 2**level)], axis=0)
        swapped = jnp.concatenate([packed[:, half:], packed[:, :half]], axis=1)
        other = jnp.concatenate([jnp.where(top, packed, swapped), jnp.where(top, swapped, packed)], axis=0)
        merged = jnp.where(halves == bit, piece, other)
        sweeps = COARSEST_SWEEPS if level == depths - 1 else COARSE_SWEEPS
        value = coarse_sweeps(weights[level], diagonals[level], merged, OMEGA * merged / diagonals[level], sweeps - 1)
        stored.append((merged, value))
        if level < depths - 1:
            rest = merged - coarse_apply(weights[level], value)
            piece = picked_sum(stack(rest), one_hot_twice(maps[0, pl.ds(level, 1)], width), NT)
    for level in reversed(range(depths)):
        merged, below = stored[level]
        if level < depths - 1:
            bit = (here >> (level + 1)) & 1
            one_hot = one_hot_rows(maps[0, pl.ds(level, 1)] + bit * half, width)
            value = below + picked_sum(stack(value), one_hot, NN)
            value = coarse_sweeps(weights[level], diagonals[level], merged, value, COARSE_SWEEPS)
    one_hot = one_hot_rows(aggregate[...] + (here & 1) * half, width)
    lifted = picked_sum(stack(value), one_hot, NN)
    for tile in range(aggregate.shape[1] // width):
        rows = pl.ds(tile * panels, panels)
        result[rows] = upper[rows] + lifted[:, tile * width:(tile + 1) * width]


def outer_devices(layout, own_tiles, wide):
    core = lax.axis_index("pair")
    here, devices = position(), lax.axis_size(AXES)
    chunks = []
    for side_name, entries in layout.items():
        is_left = (core == 0) if side_name == "out" else (core == 1)
        before = 0
        for entry in entries:
            size, distance = entry["tiles"], entry["distance"]
            start = jnp.where(is_left, wide - before - size, wide + own_tiles + before)
            base = jnp.where(is_left, wide - distance * own_tiles, wide + distance * own_tiles) - HALO
            owner = jnp.where(is_left, here - distance, here + distance)
            chunks.append(dict(
                entry, before=before, start=start, base=base, is_left=is_left,
                valid=(owner >= 0) & (owner < devices),
            ))
            before += size
    return chunks


def chunk_rows(refs, chunk, key, tile, panels):
    name, offset = chunk[key]
    if offset == "core":
        offset = lax.axis_index("pair") * (refs[name].shape[0] - HALO * panels)
        return refs[name][pl.ds(pl.multiple_of(offset + tile * panels, panels), panels)]
    if isinstance(tile, int):
        return refs[name][pl.ds(offset + tile * panels, panels)]
    return refs[name][pl.ds(pl.multiple_of(offset + tile * panels, 8), panels)]


def wide_apply(blocks, numbers, shift, base, extended, tile):
    links = blocks.shape[1]
    picked = []
    for link in range(links):
        place = base + numbers[0, shift + tile * links + link].astype(jnp.int32)
        picked.append(extended[jnp.clip(place, 0, extended.shape[0] - 1)])
    return product(jnp.concatenate(picked, axis=1), weights_of(blocks, tile), NT, blocks.shape[-1])


def chunk_diagonal(blocks, numbers, shift, chunk, tile):
    total = None
    for link in range(blocks.shape[1]):
        place = chunk["base"] + numbers[0, shift + tile * blocks.shape[1] + link].astype(jnp.int32)
        term = diagonal_row(blocks[tile, link]) * (place == chunk["start"] + tile).astype(F32)
        total = term if total is None else total + term
    return total


def wide_kernel(names, layout, panels, wide, integers_at, finish, outputs, *args):
    refs = dict(zip(names, args))
    outs = args[len(names):len(names) + outputs]
    extended, values = args[len(names) + outputs:][:2], args[len(names) + outputs:][2:4]
    diagonals, near, numbers, semaphores = args[len(names) + outputs + 4:]
    pieces = {0: [n for n in names if n.startswith("blocks_pair")], 1: [n for n in names if n.startswith("blocks_chip")]}
    blocks, own, columns = refs["blocks"], refs["vector"], refs["columns"]
    own_tiles, width = blocks.shape[0], blocks.shape[-1]
    reach = near.shape[1]
    core = lax.axis_index("pair")
    arrivals = [
        pltpu.make_async_copy(refs["integers_pair"].at[pl.ds(integers_at, 8)], numbers.at[0], semaphores.at[0]),
        pltpu.make_async_copy(refs["integers_chip"].at[pl.ds(integers_at, 8)], numbers.at[1], semaphores.at[1]),
    ]
    for which in (0, 1):
        at = 0
        for name in pieces[which]:
            size = refs[name].shape[0]
            arrivals.append(
                pltpu.make_async_copy(refs[name], near.at[which, pl.ds(at, size)], semaphores.at[len(arrivals)])
            )
            at += size
    for copy in arrivals:
        copy.start()
    chunks = outer_devices(layout, own_tiles, wide)
    for tile in range(own_tiles):
        extended[0][wide + tile] = stack(own[pl.ds(tile * panels, panels)])
    for chunk in chunks:
        for tile in range(chunk["tiles"]):
            old = jnp.where(chunk["valid"], chunk_rows(refs, chunk, "vector", tile, panels), 0.0)
            extended[0][chunk["start"] + tile] = stack(old)
    stages = wide // HALO
    fresh = []
    for stage in range(1, stages + 1):
        before, after = extended[(stage - 1) % 2], extended[stage % 2]
        past, future = values[(stage - 1) % 2], values[stage % 2]
        for tile in range(own_tiles):
            rows = pl.ds((wide + tile) * panels, panels)
            rest = get_tile(refs["source"], tile, panels, width) - tile_apply(
                columns, blocks, before, tile, wide - HALO
            )
            if stage == stages and finish == "down":
                fresh.append(rest)
                continue
            old = own[pl.ds(tile * panels, panels)] if stage == 1 else past[rows]
            new = old + OMEGA * rest / refs["diagonal"][pl.ds(tile, 1)]
            if stage < stages:
                future[rows] = new
                after[wide + tile] = stack(new)
            if stage == stages - 1 and finish == "down":
                outs[0][pl.ds(tile * panels, panels)] = new
            if stage == stages:
                if finish == "up":
                    prolong(tile, new, refs["aggregate"], refs["upper"], panels, width, own_tiles, outs[0])
                else:
                    put_tile(outs[0], tile, new, panels, width)
        if stage == 1:
            for copy in arrivals:
                copy.wait()
        for chunk in chunks:
            count = min(max(wide - HALO * stage - chunk["before"], 0), chunk["tiles"])
            first = jnp.where(chunk["is_left"], chunk["tiles"] - count, 0)
            for k in range(count):
                tile = k if count == chunk["tiles"] else first + k
                place = chunk["start"] + tile
                rows = pl.ds(pl.multiple_of(place * panels, panels), panels)
                which, shift = chunk["columns"]
                rest = chunk_rows(refs, chunk, "source", tile, panels) - wide_apply(
                    near.at[which], numbers.at[which], shift, chunk["base"], before, tile
                )
                if stage == 1:
                    row = chunk_diagonal(near.at[which], numbers.at[which], shift, chunk, tile)
                    if stages > 2:
                        diagonals[which * reach + tile] = jnp.broadcast_to(row, (8, width))
                    old = chunk_rows(refs, chunk, "vector", tile, panels)
                else:
                    row = diagonals[which * reach + tile][:1]
                    old = past[rows]
                new = jnp.where(chunk["valid"], old + OMEGA * rest / row, 0.0)
                if stage < stages - 1:
                    future[rows] = new
                after[place] = stack(new)
    if finish == "down":
        restrict(fresh, refs["aggregate"], refs["next_columns"], refs["next_blocks"], panels, *outs[1:4])
    if finish == "up":
        put_wide_edges(outs[0], outs[0].shape[0] // panels, panels, wide, outs[1], outs[2])


def call(kernel, shapes, operands, scalars=(), remote=(), scratch=(), name=None, carry=(), tokens=(), limit=VMEM_BYTES):
    vmem = pl.BlockSpec(memory_space=pltpu.VMEM)
    smem = pl.BlockSpec(memory_space=pltpu.SMEM)
    free = pl.BlockSpec(memory_space=pl.ANY)
    specs = [smem if k in scalars else free if k in remote else vmem for k in range(len(operands))]
    taken, given, count = len(operands), len(shapes), len(carry)

    def body(*refs):
        ins, origins, refs = refs[:taken], refs[taken:taken + count], refs[taken + count + len(tokens):]
        outs, copied, rest = refs[:given], refs[given:given + count], refs[given + count:]
        copies = [
            pltpu.make_async_copy(origin.at[pl.ds(first, size)], target, rest[-1].at[k])
            for k, (origin, (_, first, size), target) in enumerate(zip(origins, carry_firsts(), copied))
        ]
        for copy in copies:
            copy.start()
        kernel(*ins, *outs, *(rest[:-1] if count else rest))
        for copy in copies:
            copy.wait()

    def carry_firsts():
        return [(array, first() if callable(first) else first, size) for array, first, size in carry]

    extra = [jax.ShapeDtypeStruct((size,) + array.shape[1:], array.dtype) for array, _, size in carry]
    return pl.pallas_call(
        body,
        out_shape=[jax.ShapeDtypeStruct(s, t) for s, t in shapes] + extra,
        in_specs=specs + [free] * (count + len(tokens)),
        out_specs=[vmem] * given + [free] * count,
        scratch_shapes=list(scratch) + ([pltpu.SemaphoreType.DMA((count,))] if count else []),
        compiler_params=pltpu.CompilerParams(vmem_limit_bytes=limit),
        name=name,
    )(*operands, *[array for array, _, _ in carry], *tokens)


def swaps(pairs):
    return [p for a, b in pairs for p in ((a, b), (b, a))]


def inner_swap(value):
    count = lax.axis_size(AXES)
    return lax.ppermute(value, AXES, swaps([(2 * k, 2 * k + 1) for k in range(count // 2)]))


def outer_swap(value):
    count = lax.axis_size(AXES)
    return lax.ppermute(value, AXES, swaps([(2 * k + 1, 2 * k + 2) for k in range(count // 2 - 1)]))


def exchange(pair_edge, chip_edge):
    return inner_swap(pair_edge), outer_swap(chip_edge)


def side(tiles, distance, vector, source=None, columns=None):
    entry = dict(tiles=tiles, distance=distance, vector=vector)
    if source is not None:
        entry.update(source=source, columns=columns)
    return entry


def on_device(
    pulse_rhs, blocks_fine, columns_fine, aggregate_fine, blocks_mid, columns_mid, aggregate_mid,
    blocks_low, columns_low, aggregate_low, coarse_ops, coarse_maps,
):
    panels, width = pulse_rhs.shape[0], blocks_fine.shape[-1]
    devices = lax.axis_size(AXES)
    blocks = (blocks_fine, blocks_mid, blocks_low)
    columns = (columns_fine.T, columns_mid, columns_low)
    aggregates = tuple(a.reshape(1, -1) for a in (aggregate_fine, aggregate_mid, aggregate_low))
    counts = tuple(b.shape[0] for b in blocks)
    depths = coarse_ops.shape[1]
    wide = (6, 6)
    reach = tuple(w - HALO for w in wide)
    edge_rows = HALO * panels

    def rows(tiles, extra=0):
        return ((tiles * panels + extra, width), F32)

    def vec(level):
        return rows(counts[level])

    def diag(level):
        return ((counts[level], width), F32)

    def ext(level):
        return [pltpu.VMEM((counts[level] + 2 * HALO, 2 * panels, width), BF16)]

    def wide_call(level, finish, layout, shapes, operands, integers, near_pair, near_chip, step):
        operands = dict(
            operands, source=sources[level], diagonal=diagonals[level], blocks=blocks[level], columns=columns[level],
            integers_pair=integers[0], integers_chip=integers[1], blocks_pair=near_pair,
            **{f"blocks_chip{k}": piece for k, piece in enumerate(near_chip)},
        )
        names = tuple(operands)
        count = counts[level] + 2 * wide[level]
        return step(
            f"wide_{finish}{level}", functools.partial(wide_kernel, names, layout, panels, wide[level], integers[2], finish, len(shapes)),
            shapes, tuple(operands[k] for k in names),
            scalars=tuple(k for k, name in enumerate(names) if "columns" in name),
            remote=tuple(k for k, name in enumerate(names) if name.startswith(("integers", "blocks_"))),
            scratch=[pltpu.VMEM((count, 2 * panels, width), BF16)] * 2
            + [pltpu.VMEM((count * panels, width), F32)] * 2
            + [
                pltpu.VMEM((2 * reach[level], 8, width), F32),
                pltpu.VMEM((2, reach[level]) + blocks_fine.shape[1:], F32),
                pltpu.SMEM((2, 8, width), F32),
                pltpu.SemaphoreType.DMA((3 + len(near_chip),)),
            ],
        )

    def facing(towards_pair, tile):
        def first():
            core = lax.axis_index("pair")
            return (1 - core if towards_pair else core) * (counts[0] - reach[0]) + tile
        return first

    pieces_of = {
        **{f"mid{k}": (blocks_mid, k, 1) for k in range(counts[1])},
        **{f"fine{k}": (blocks_fine, facing(False, k), 1) for k in range(reach[0])},
    }
    arrived = {}

    def step(name, kernel, shapes, operands, tokens=(), **more):
        leaving = LEAVE.get(name, ())
        outs = call(
            kernel, shapes, operands, name=name, carry=[pieces_of[p] for p in leaving],
            tokens=[arrived[p] for p in ARRIVE.get(name, ())] + list(tokens), **more,
        )
        pieces = dict(zip(leaving, outs[len(shapes):]))
        return outs[:len(shapes)], lambda: arrived.update({p: outer_swap(v) for p, v in pieces.items()})

    mid_pair = inner_swap(blocks_mid)
    images = call(maps_kernel, [((width // 2, 2 * depths * width), BF16)], (coarse_ops, coarse_maps), name="maps")[0]

    first_edge = rows(HALO + reach[0], 8)
    (diagonal, vector, pair_edge, chip_edge), leave = step(
        "first", functools.partial(first_kernel, reach[0]), [diag(0), vec(0), first_edge, first_edge],
        (columns[0], pulse_rhs, blocks_fine), scalars=(0,),
    )
    sources, diagonals = [pulse_rhs], [diagonal]
    halos = first_halos = exchange(pair_edge, chip_edge)
    leave()
    for k in range(2):
        (vector, pair_edge, chip_edge), leave = step(
            f"sweep0{k}", functools.partial(sweep_kernel, panels, True), [vec(0), rows(HALO), rows(HALO)],
            (columns[0], vector, *halos, pulse_rhs, diagonal, blocks_fine), scalars=(0,), scratch=ext(0),
        )
        halos = exchange(pair_edge, chip_edge)
        leave()
    kept = [vector]
    fine_pair = call(copy_kernel, [], (), name="near", carry=[(blocks_fine, facing(True, 0), reach[0])])[0]
    fine_pair = inner_swap(fine_pair)
    (source, diagonal, vector, packed), leave = step(
        "residual0", functools.partial(residual_kernel, panels),
        [vec(1), diag(1), vec(1), rows(2 * counts[1] + HALO, 8)],
        (columns[0], vector, *halos, pulse_rhs, blocks_fine, aggregates[0], columns_mid, blocks_mid),
        scalars=(0, 7), scratch=ext(0),
    )
    sources.append(source)
    diagonals.append(diagonal)

    size = counts[1] * panels
    pair = inner_swap(packed)
    chip = outer_swap(jnp.concatenate([packed[:2 * size + 8], pair[2 * size + 8:]]))
    leave()
    far = inner_swap(chip[:size])
    first_mid = (pair, chip, 2 * size)

    def mid_layout(second):
        return {
            "out": [side(counts[1], 1, ("chip", 0), ("chip_source", size), (1, 0)), side(HALO, 1, ("chip", second))],
            "in": [side(counts[1], 1, ("pair", 0), ("pair_source", size), (0, 0)), side(HALO, 1, ("far", "core"))],
        }

    mid_chip = [arrived[f"mid{k}"] for k in range(counts[1])]
    (vector, source, diagonal, next_vector), leave = wide_call(
        1, "down", mid_layout(2 * size + 8), [vec(1), vec(2), diag(2), vec(2)],
        dict(vector=vector, pair=pair, chip=chip, far=far, pair_source=pair, chip_source=chip,
             aggregate=aggregates[1], next_columns=columns_low, next_blocks=blocks_low),
        first_mid, mid_pair, mid_chip, step,
    )
    kept.append(vector)
    sources.append(source)
    diagonals.append(diagonal)

    vector = next_vector
    halos = exchange(vector, vector)
    leave()

    def sweep_low(name, vector, halos):
        (vector,), leave = step(
            name, functools.partial(sweep_kernel, panels, False), [vec(2)],
            (columns_low, vector, *halos, sources[2], diagonals[2], blocks_low), scalars=(0,), scratch=ext(2),
        )
        halos = exchange(vector, vector)
        leave()
        return vector, halos

    for k in range(2):
        vector, halos = sweep_low(f"down2{k}", vector, halos)
    (own_piece, outgoing), _ = step(
        "lowest", functools.partial(lowest_kernel, panels),
        [((panels, width), F32), ((devices, panels // 2, width), F32)],
        (columns_low, vector, *halos, sources[2], blocks_low, aggregates[2], images),
        scalars=(0,), scratch=ext(2), tokens=[fine_pair],
    )
    incoming = lax.all_to_all(outgoing, AXES, 0, 0)
    (vector,), leave = step(
        "chain", functools.partial(chain_kernel, panels), [vec(2)],
        (own_piece, incoming, coarse_ops, coarse_maps, aggregates[2], vector),
    )
    halos = exchange(vector, vector)
    leave()
    for k in range(2):
        vector, halos = sweep_low(f"up2{k}", vector, halos)
    (vector, packed), leave = step(
        "prolong2", functools.partial(prolong_kernel, panels), [vec(1), rows(counts[1] + HALO)],
        (columns_low, vector, *halos, sources[2], diagonals[2], blocks_low, aggregates[1], kept[1]),
        scalars=(0,), scratch=ext(2),
    )

    pair = inner_swap(packed)
    chip = outer_swap(jnp.concatenate([vector, pair[size:]]))
    leave()
    far = inner_swap(chip[:size])
    (vector, pair_edge, chip_edge), leave = wide_call(
        1, "up", mid_layout(size), [vec(0), rows(wide[0]), rows(wide[0])],
        dict(vector=vector, pair=pair, chip=chip, far=far, pair_source=first_mid[0], chip_source=first_mid[1],
             aggregate=aggregates[0], upper=kept[0]),
        first_mid, mid_pair, mid_chip, step,
    )

    pair, chip = exchange(pair_edge, chip_edge)
    layout = {
        name: [side(reach[0], 1, (array, 0), (array + "_source", edge_rows + 8), (which, 0)),
               side(HALO, 1, (array, reach[0] * panels))]
        for name, array, which in (("out", "chip", 1), ("in", "pair", 0))
    }
    return wide_call(
        0, "last", layout, [(pulse_rhs.shape, F32)],
        dict(vector=vector, pair=pair, chip=chip, pair_source=first_halos[0], chip_source=first_halos[1]),
        (*first_halos, edge_rows), fine_pair, [arrived[f"fine{k}"] for k in range(reach[0])], step,
    )[0][0]


LEAVE = {'first': ('mid0', 'mid1'), 'sweep00': ('mid2',), 'sweep01': ('mid3',), 'wide_down1': ('fine0',), 'chain': ('fine1',), 'up20': ('fine2',), 'up21': ('fine3',)}
ARRIVE = {'sweep01': ('mid0', 'mid1'), 'residual0': ('mid2',), 'down21': ('fine0',), 'up21': ('fine1',), 'prolong2': ('fine2',)}


def solution(mesh):
    split_first = P(AXES)
    rhs = P(None, AXES)
    return jax.shard_map(
        on_device, mesh=mesh, in_specs=(rhs,) + (split_first,) * 11, out_specs=rhs, check_vma=False
    )
```

```python
import functools

import jax
import jax.numpy as jnp
from jax import lax
from jax.experimental import pallas as pl
from jax.experimental.pallas import tpu as pltpu
from jax.sharding import PartitionSpec as P

HALO = 2
VMEM_BYTES = 24 * 2**20
COARSE_SWEEPS = 2
COARSEST_SWEEPS = 8
OMEGA = 0.7
AXES = ("parts", "pair")
NT = (((1,), (1,)), ((), ()))
NN = (((1,), (0,)), ((), ()))
F32 = jnp.float32
BF16 = jnp.bfloat16


def split(value):
    high = value.astype(BF16)
    return high, (value - high.astype(F32)).astype(BF16)


def stack(value):
    return jnp.concatenate(split(value), axis=0)


def fold_rows(value):
    half = value.shape[0] // 2
    return value[:half] + value[half:]


def product(stacked, weights, dims, width):
    full = lax.dot_general(stacked, weights, dims, preferred_element_type=F32)
    rows = full.shape[0] // 2
    return full[:rows, :width] + (full[:rows, width:] + full[rows:, :width])


def picked_sum(stacked, one_hot, dims):
    return fold_rows(lax.dot_general(stacked, one_hot, dims, preferred_element_type=F32))


def position():
    return lax.axis_index("parts") * lax.axis_size("pair") + lax.axis_index("pair")


def diagonal_row(block):
    size = block.shape[-1]
    rows = lax.broadcasted_iota(jnp.int32, (size, size), 0)
    lanes = lax.broadcasted_iota(jnp.int32, (size, size), 1)
    return jnp.sum(jnp.where(rows == lanes, block, 0.0), axis=0, keepdims=True)


def column(columns, blocks, tile, link):
    if columns.shape == blocks.shape[:2]:
        return columns[tile, link]
    return columns[link, tile]


def tile_diagonal(columns, blocks, tile):
    total = None
    for link in range(blocks.shape[1]):
        own = (column(columns, blocks, tile, link) == tile + HALO).astype(F32)
        term = diagonal_row(blocks[tile, link]) * own
        total = term if total is None else total + term
    return total


def get_tile(ref, tile, panels, width):
    if ref.shape[0] == panels:
        return ref[:, tile * width:(tile + 1) * width]
    return ref[pl.ds(tile * panels, panels)]


def put_tile(ref, tile, value, panels, width):
    if ref.shape[0] == panels and ref.shape[1] != width:
        ref[:, tile * width:(tile + 1) * width] = value
    else:
        ref[pl.ds(tile * panels, panels)] = value


def fill_extended(extended, vector, pair_halo, chip_halo, count, panels):
    core = lax.axis_index("pair")
    for tile in range(count):
        extended[tile + HALO] = stack(vector[pl.ds(tile * panels, panels)])
    for tile in range(HALO):
        rows = pl.ds(tile * panels, panels)
        extended[core * (count + HALO) + tile] = stack(chip_halo[rows])
        extended[(1 - core) * (count + HALO) + tile] = stack(pair_halo[rows])


def dims(blocks):
    if len(blocks.shape) == 4:
        return blocks.shape[0], blocks.shape[1], blocks.shape[-1]
    return blocks.shape[0], 2 * blocks.shape[1] // blocks.shape[2], blocks.shape[2] // 2


def prepare_kernel(blocks_hbm, weights, blocks, semaphores):
    count, links, width = blocks.shape[0], blocks.shape[1], blocks.shape[-1]
    chunks = semaphores.shape[0]
    size = count // chunks
    copies = [
        pltpu.make_async_copy(blocks_hbm.at[pl.ds(k * size, size)], blocks.at[pl.ds(k * size, size)], semaphores.at[k])
        for k in range(chunks)
    ]
    for copy in copies:
        copy.start()
    for tile in range(count):
        if tile % size == 0:
            copies[tile // size].wait()
        for link in range(links):
            high, low = split(blocks[tile, link].T)
            rows = slice(link * width, (link + 1) * width)
            weights[tile, rows, :width] = high
            weights[tile, rows, width:] = low


def weights_of(blocks, tile):
    parts = [split(blocks[tile, k]) for k in range(blocks.shape[1])]
    return jnp.concatenate(
        [jnp.concatenate([p[0] for p in parts], axis=1), jnp.concatenate([p[1] for p in parts], axis=1)], axis=0
    )


def tile_apply(columns, blocks, extended, tile, shift=0):
    _, links, width = dims(blocks)
    picked = jnp.concatenate([extended[column(columns, blocks, tile, k) + shift] for k in range(links)], axis=1)
    if len(blocks.shape) == 3:
        return product(picked, blocks[tile], NN, width)
    return product(picked, weights_of(blocks, tile), NT, width)


def put_edges(vector, count, panels, pair_edge, chip_edge):
    core = lax.axis_index("pair")
    last = (count - HALO) * panels
    size = HALO * panels
    pair_edge[pl.ds(0, size)] = vector[pl.ds(pl.multiple_of((1 - core) * last, panels), size)]
    chip_edge[pl.ds(0, size)] = vector[pl.ds(pl.multiple_of(core * last, panels), size)]


def put_wide_edges(vector, count, panels, wide, pair_edge, chip_edge):
    core = lax.axis_index("pair")
    reach = wide - HALO
    for edge, turn in ((pair_edge, 1 - core), (chip_edge, core)):
        near = pl.multiple_of(turn * (count - reach) * panels, panels)
        far = pl.multiple_of(jnp.where(turn == 1, count - wide, reach) * panels, panels)
        edge[pl.ds(0, reach * panels)] = vector[pl.ds(near, reach * panels)]
        edge[pl.ds(reach * panels, HALO * panels)] = vector[pl.ds(far, HALO * panels)]


def integer_row(values, width):
    lanes = lax.broadcasted_iota(jnp.int32, (8, width), 1)
    row = jnp.zeros((8, width), F32)
    for k, value in enumerate(values):
        row = jnp.where(lanes == k, value.astype(F32), row)
    return row


def columns_row(columns, blocks, first, tiles, width):
    links = blocks.shape[1]
    return integer_row([column(columns, blocks, first + t, k) for t in range(tiles) for k in range(links)], width)


def first_kernel(
    reach, columns, source, blocks_hbm, diagonal, vector, pair_edge, chip_edge, blocks, semaphores
):
    panels = source.shape[0]
    count, width = blocks.shape[0], blocks.shape[-1]
    core = lax.axis_index("pair")
    start = HALO * panels
    chunks = semaphores.shape[0]
    size = count // chunks
    copies = [
        pltpu.make_async_copy(blocks_hbm.at[pl.ds(k * size, size)], blocks.at[pl.ds(k * size, size)], semaphores.at[k])
        for k in range(chunks)
    ]
    for copy in copies:
        copy.start()
    for edge, turn in ((pair_edge, 1 - core), (chip_edge, core)):
        edge[pl.ds(start, 8)] = columns_row(columns, blocks, turn * (count - reach), reach, width)
        for tile in range(reach):
            ahead, behind = get_tile(source, tile, panels, width), get_tile(source, count - reach + tile, panels, width)
            edge[pl.ds(start + 8 + tile * panels, panels)] = jnp.where(turn == 1, behind, ahead)
    for tile in range(count):
        if tile % size == 0:
            copies[tile // size].wait()
        row = tile_diagonal(columns, blocks, tile)
        diagonal[pl.ds(tile, 1)] = row
        vector[pl.ds(tile * panels, panels)] = OMEGA * get_tile(source, tile, panels, width) / row
    put_edges(vector, count, panels, pair_edge, chip_edge)


def copy_kernel(*_):
    pass


def sweep_kernel(panels, edges, columns, vector, pair_halo, chip_halo, source, diagonal, blocks, result, *rest):
    extended = rest[-1]
    count, _, width = dims(blocks)
    fill_extended(extended, vector, pair_halo, chip_halo, count, panels)
    for tile in range(count):
        product_tile = tile_apply(columns, blocks, extended, tile)
        old = vector[pl.ds(tile * panels, panels)]
        new = old + OMEGA * (get_tile(source, tile, panels, width) - product_tile) / diagonal[pl.ds(tile, 1)]
        put_tile(result, tile, new, panels, width)
    if edges:
        put_edges(result, count, panels, rest[0], rest[1])


def restrict(pieces, aggregate, next_columns, next_blocks, panels, next_source, next_diagonal, next_vector):
    width, next_count = next_blocks.shape[-1], next_blocks.shape[0]
    factor = len(pieces) // next_count
    for group in range(next_count):
        one_hot = one_hot_rows(aggregate[:, group * factor * width:(group + 1) * factor * width], width)
        stacked = jnp.concatenate([stack(p) for p in pieces[group * factor:(group + 1) * factor]], axis=1)
        gathered = picked_sum(stacked, one_hot, NT)
        row = tile_diagonal(next_columns, next_blocks, group)
        rows = pl.ds(group * panels, panels)
        next_source[rows] = gathered
        next_diagonal[pl.ds(group, 1)] = row
        next_vector[rows] = OMEGA * gathered / row


def residual_kernel(
    panels, columns, vector, pair_halo, chip_halo, source, blocks, aggregate, next_columns, next_blocks,
    next_source, next_diagonal, next_vector, packed, extended,
):
    count, _, width = dims(blocks)
    fill_extended(extended, vector, pair_halo, chip_halo, count, panels)
    pieces = [
        get_tile(source, tile, panels, width) - tile_apply(columns, blocks, extended, tile) for tile in range(count)
    ]
    restrict(pieces, aggregate, next_columns, next_blocks, panels, next_source, next_diagonal, next_vector)
    put_packed(packed, next_vector, panels, next_source, next_columns, next_blocks)


def put_packed(packed, vector, panels, source=None, columns=None, blocks=None):
    size, width = vector.shape
    packed[pl.ds(0, size)] = vector[...]
    at = size
    if source is not None:
        packed[pl.ds(at, size)] = source[...]
        packed[pl.ds(at + size, 8)] = columns_row(columns, blocks, 0, blocks.shape[0], width)
        at += size + 8
    if packed.shape[0] > at:
        edge = HALO * panels
        first = pl.multiple_of((1 - lax.axis_index("pair")) * (size - edge), panels)
        packed[pl.ds(at, edge)] = vector[pl.ds(first, edge)]


def one_hot_rows(indices, width):
    rows = lax.broadcasted_iota(jnp.int32, (width, indices.shape[1]), 0)
    return (rows == indices).astype(F32).astype(BF16)


def one_hot_twice(indices, width):
    rows = lax.broadcasted_iota(jnp.int32, (width, indices.shape[1]), 0)
    half = width // 2
    return (jnp.where(rows < half, rows, rows - half) == indices).astype(F32).astype(BF16)


def prolong(tile, value, aggregate, upper, panels, width, own_tiles, result):
    factor = upper.shape[0] // panels // own_tiles
    one_hot = one_hot_rows(aggregate[:, tile * factor * width:(tile + 1) * factor * width], width)
    lifted = picked_sum(stack(value), one_hot, NN)
    for k in range(factor):
        rows = pl.ds((tile * factor + k) * panels, panels)
        result[rows] = upper[rows] + lifted[:, k * width:(k + 1) * width]


def prolong_kernel(
    panels, columns, vector, pair_halo, chip_halo, source, diagonal, blocks, aggregate, upper,
    next_vector, packed, extended,
):
    count, width = blocks.shape[0], blocks.shape[-1]
    fill_extended(extended, vector, pair_halo, chip_halo, count, panels)
    for tile in range(count):
        product_tile = tile_apply(columns, blocks, extended, tile)
        old = vector[pl.ds(tile * panels, panels)]
        new = old + OMEGA * (get_tile(source, tile, panels, width) - product_tile) / diagonal[pl.ds(tile, 1)]
        prolong(tile, new, aggregate, upper, panels, width, count, next_vector)
    put_packed(packed, next_vector, panels)


def chain_weights(operators, depths):
    weights, diagonals = [], []
    for level in range(depths):
        matrix = operators[0, level]
        weights.append(jnp.concatenate(split(matrix), axis=0))
        diagonals.append(diagonal_row(matrix))
    return weights, diagonals


def coarse_apply(weights, value):
    return product(stack(value), weights, NT, value.shape[1])


def coarse_sweeps(weights, diagonal, source, value, sweeps):
    for _ in range(sweeps):
        value = value + OMEGA * (source - coarse_apply(weights, value)) / diagonal
    return value


def lane_half(rows, width):
    return (lax.broadcasted_iota(jnp.int32, (rows, width), 1) >= width // 2).astype(jnp.int32)


def maps_kernel(operators, maps, result):
    depths, width = operators.shape[1], operators.shape[-1]
    half = width // 2
    here = position()
    weights, diagonals = chain_weights(operators, depths - 1)
    lanes = lax.broadcasted_iota(jnp.int32, (half, width), 1)
    rows = lax.broadcasted_iota(jnp.int32, (half, width), 0)
    piece = (jnp.where(lanes < half, lanes, lanes - half) == rows).astype(F32)
    halves = lane_half(half, width)
    for level in range(depths):
        high, low = split(piece)
        result[:, 2 * level * width:(2 * level + 1) * width] = high
        result[:, (2 * level + 1) * width:(2 * level + 2) * width] = low
        if level < depths - 1:
            bit = (here >> level) & 1
            merged = jnp.where(halves == bit, piece, 0.0)
            value = coarse_sweeps(
                weights[level], diagonals[level], merged, OMEGA * merged / diagonals[level], COARSE_SWEEPS - 1
            )
            rest = merged - coarse_apply(weights[level], value)
            piece = picked_sum(stack(rest), one_hot_twice(maps[0, pl.ds(level, 1)], width), NT)


def send_shares(pieces, aggregate, images, panels, own_piece, outgoing):
    width = own_piece.shape[1]
    half = width // 2
    here = position()
    one_hot = one_hot_twice(aggregate[...], width)
    gathered = picked_sum(jnp.concatenate(pieces, axis=1), one_hot, NT)
    own_piece[...] = gathered
    shares = lax.dot_general(stack(gathered)[:, :half], images[...], NN, preferred_element_type=F32)
    depths = images.shape[1] // (2 * width)
    top = lax.broadcasted_iota(jnp.int32, (panels // 2, width), 1) < half
    for level in range(depths):
        low = shares[:, 2 * level * width:(2 * level + 2) * width]
        share = low[:panels, :width] + (low[:panels, width:] + low[panels:, :width])
        packed = jnp.where(top, share[:panels // 2], share[panels // 2:])
        start = ((here >> level) ^ 1) << level
        if level == 0:
            outgoing[pl.ds(here, 1)] = packed[None]
        outgoing[pl.ds(start, 2**level)] = jnp.broadcast_to(packed[None], (2**level,) + packed.shape)


def lowest_kernel(
    panels, columns, vector, pair_halo, chip_halo, source, blocks, aggregate, images,
    own_piece, outgoing, extended,
):
    count, width = blocks.shape[0], blocks.shape[-1]
    fill_extended(extended, vector, pair_halo, chip_halo, count, panels)
    pieces = []
    for tile in range(count):
        rest = get_tile(source, tile, panels, width) - tile_apply(columns, blocks, extended, tile)
        pieces.append(stack(rest))
    send_shares(pieces, aggregate, images, panels, own_piece, outgoing)


def chain_kernel(panels, own_piece, incoming, operators, maps, aggregate, upper, result):
    depths, width = operators.shape[1], operators.shape[-1]
    half = width // 2
    here = position()
    weights, diagonals = chain_weights(operators, depths)
    halves = lane_half(panels, width)
    top = lax.broadcasted_iota(jnp.int32, (panels // 2, width), 1) < half
    piece = own_piece[...]
    stored = []
    for level in range(depths):
        bit = (here >> level) & 1
        start = ((here >> level) ^ 1) << level
        packed = jnp.sum(incoming[pl.ds(start, 2**level)], axis=0)
        swapped = jnp.concatenate([packed[:, half:], packed[:, :half]], axis=1)
        other = jnp.concatenate([jnp.where(top, packed, swapped), jnp.where(top, swapped, packed)], axis=0)
        merged = jnp.where(halves == bit, piece, other)
        sweeps = COARSEST_SWEEPS if level == depths - 1 else COARSE_SWEEPS
        value = coarse_sweeps(weights[level], diagonals[level], merged, OMEGA * merged / diagonals[level], sweeps - 1)
        stored.append((merged, value))
        if level < depths - 1:
            rest = merged - coarse_apply(weights[level], value)
            piece = picked_sum(stack(rest), one_hot_twice(maps[0, pl.ds(level, 1)], width), NT)
    for level in reversed(range(depths)):
        merged, below = stored[level]
        if level < depths - 1:
            bit = (here >> (level + 1)) & 1
            one_hot = one_hot_rows(maps[0, pl.ds(level, 1)] + bit * half, width)
            value = below + picked_sum(stack(value), one_hot, NN)
            value = coarse_sweeps(weights[level], diagonals[level], merged, value, COARSE_SWEEPS)
    one_hot = one_hot_rows(aggregate[...] + (here & 1) * half, width)
    lifted = picked_sum(stack(value), one_hot, NN)
    for tile in range(aggregate.shape[1] // width):
        rows = pl.ds(tile * panels, panels)
        result[rows] = upper[rows] + lifted[:, tile * width:(tile + 1) * width]


def outer_devices(layout, own_tiles, wide):
    core = lax.axis_index("pair")
    here, devices = position(), lax.axis_size(AXES)
    chunks = []
    for side_name, entries in layout.items():
        is_left = (core == 0) if side_name == "out" else (core == 1)
        before = 0
        for entry in entries:
            size, distance = entry["tiles"], entry["distance"]
            start = jnp.where(is_left, wide - before - size, wide + own_tiles + before)
            base = jnp.where(is_left, wide - distance * own_tiles, wide + distance * own_tiles) - HALO
            owner = jnp.where(is_left, here - distance, here + distance)
            chunks.append(dict(
                entry, before=before, start=start, base=base, is_left=is_left,
                valid=(owner >= 0) & (owner < devices),
            ))
            before += size
    return chunks


def chunk_rows(refs, chunk, key, tile, panels):
    name, offset = chunk[key]
    if offset == "core":
        offset = lax.axis_index("pair") * (refs[name].shape[0] - HALO * panels)
        return refs[name][pl.ds(pl.multiple_of(offset + tile * panels, panels), panels)]
    if isinstance(tile, int):
        return refs[name][pl.ds(offset + tile * panels, panels)]
    return refs[name][pl.ds(pl.multiple_of(offset + tile * panels, 8), panels)]


def wide_apply(blocks, numbers, shift, base, extended, tile):
    links = blocks.shape[1]
    picked = []
    for link in range(links):
        place = base + numbers[0, shift + tile * links + link].astype(jnp.int32)
        picked.append(extended[jnp.clip(place, 0, extended.shape[0] - 1)])
    return product(jnp.concatenate(picked, axis=1), weights_of(blocks, tile), NT, blocks.shape[-1])


def chunk_diagonal(blocks, numbers, shift, chunk, tile):
    total = None
    for link in range(blocks.shape[1]):
        place = chunk["base"] + numbers[0, shift + tile * blocks.shape[1] + link].astype(jnp.int32)
        term = diagonal_row(blocks[tile, link]) * (place == chunk["start"] + tile).astype(F32)
        total = term if total is None else total + term
    return total


def wide_kernel(names, layout, panels, wide, integers_at, finish, outputs, *args):
    refs = dict(zip(names, args))
    outs = args[len(names):len(names) + outputs]
    extended, values = args[len(names) + outputs:][:2], args[len(names) + outputs:][2:4]
    diagonals, near, numbers, semaphores = args[len(names) + outputs + 4:]
    pieces = {0: [n for n in names if n.startswith("blocks_pair")], 1: [n for n in names if n.startswith("blocks_chip")]}
    blocks, own, columns = refs["blocks"], refs["vector"], refs["columns"]
    own_tiles, _, width = dims(blocks)
    reach = near.shape[1]
    core = lax.axis_index("pair")
    arrivals = [
        pltpu.make_async_copy(refs["integers_pair"].at[pl.ds(integers_at, 8)], numbers.at[0], semaphores.at[0]),
        pltpu.make_async_copy(refs["integers_chip"].at[pl.ds(integers_at, 8)], numbers.at[1], semaphores.at[1]),
    ]
    for which in (0, 1):
        at = 0
        for name in pieces[which]:
            size = refs[name].shape[0]
            arrivals.append(
                pltpu.make_async_copy(refs[name], near.at[which, pl.ds(at, size)], semaphores.at[len(arrivals)])
            )
            at += size
    for copy in arrivals:
        copy.start()
    chunks = outer_devices(layout, own_tiles, wide)
    for tile in range(own_tiles):
        extended[0][wide + tile] = stack(own[pl.ds(tile * panels, panels)])
    for chunk in chunks:
        for tile in range(chunk["tiles"]):
            old = jnp.where(chunk["valid"], chunk_rows(refs, chunk, "vector", tile, panels), 0.0)
            extended[0][chunk["start"] + tile] = stack(old)
    stages = wide // HALO
    fresh = []
    for stage in range(1, stages + 1):
        before, after = extended[(stage - 1) % 2], extended[stage % 2]
        past, future = values[(stage - 1) % 2], values[stage % 2]
        for tile in range(own_tiles):
            rows = pl.ds((wide + tile) * panels, panels)
            rest = get_tile(refs["source"], tile, panels, width) - tile_apply(
                columns, blocks, before, tile, wide - HALO
            )
            if stage == stages and finish == "down":
                fresh.append(rest)
                continue
            old = own[pl.ds(tile * panels, panels)] if stage == 1 else past[rows]
            new = old + OMEGA * rest / refs["diagonal"][pl.ds(tile, 1)]
            if stage < stages:
                future[rows] = new
                after[wide + tile] = stack(new)
            if stage == stages - 1 and finish == "down":
                outs[0][pl.ds(tile * panels, panels)] = new
            if stage == stages:
                if finish == "up":
                    prolong(tile, new, refs["aggregate"], refs["upper"], panels, width, own_tiles, outs[0])
                else:
                    put_tile(outs[0], tile, new, panels, width)
        if stage == 1:
            for copy in arrivals:
                copy.wait()
        for chunk in chunks:
            count = min(max(wide - HALO * stage - chunk["before"], 0), chunk["tiles"])
            first = jnp.where(chunk["is_left"], chunk["tiles"] - count, 0)
            for k in range(count):
                tile = k if count == chunk["tiles"] else first + k
                place = chunk["start"] + tile
                rows = pl.ds(pl.multiple_of(place * panels, panels), panels)
                which, shift = chunk["columns"]
                rest = chunk_rows(refs, chunk, "source", tile, panels) - wide_apply(
                    near.at[which], numbers.at[which], shift, chunk["base"], before, tile
                )
                if stage == 1:
                    row = chunk_diagonal(near.at[which], numbers.at[which], shift, chunk, tile)
                    if stages > 2:
                        diagonals[which * reach + tile] = jnp.broadcast_to(row, (8, width))
                    old = chunk_rows(refs, chunk, "vector", tile, panels)
                else:
                    row = diagonals[which * reach + tile][:1]
                    old = past[rows]
                new = jnp.where(chunk["valid"], old + OMEGA * rest / row, 0.0)
                if stage < stages - 1:
                    future[rows] = new
                after[place] = stack(new)
    if finish == "down":
        restrict(fresh, refs["aggregate"], refs["next_columns"], refs["next_blocks"], panels, *outs[1:4])
    if finish == "up":
        put_wide_edges(outs[0], outs[0].shape[0] // panels, panels, wide, outs[1], outs[2])


def call(kernel, shapes, operands, scalars=(), remote=(), scratch=(), name=None, carry=(), tokens=(), limit=VMEM_BYTES):
    vmem = pl.BlockSpec(memory_space=pltpu.VMEM)
    smem = pl.BlockSpec(memory_space=pltpu.SMEM)
    free = pl.BlockSpec(memory_space=pl.ANY)
    specs = [smem if k in scalars else free if k in remote else vmem for k in range(len(operands))]
    taken, given, count = len(operands), len(shapes), len(carry)

    def body(*refs):
        ins, origins, refs = refs[:taken], refs[taken:taken + count], refs[taken + count + len(tokens):]
        outs, copied, rest = refs[:given], refs[given:given + count], refs[given + count:]
        copies = [
            pltpu.make_async_copy(origin.at[pl.ds(first, size)], target, rest[-1].at[k])
            for k, (origin, (_, first, size), target) in enumerate(zip(origins, carry_firsts(), copied))
        ]
        for copy in copies:
            copy.start()
        kernel(*ins, *outs, *(rest[:-1] if count else rest))
        for copy in copies:
            copy.wait()

    def carry_firsts():
        return [(array, first() if callable(first) else first, size) for array, first, size in carry]

    extra = [jax.ShapeDtypeStruct((size,) + array.shape[1:], array.dtype) for array, _, size in carry]
    return pl.pallas_call(
        body,
        out_shape=[jax.ShapeDtypeStruct(s, t) for s, t in shapes] + extra,
        in_specs=specs + [free] * (count + len(tokens)),
        out_specs=[vmem] * (given + count),
        scratch_shapes=list(scratch) + ([pltpu.SemaphoreType.DMA((count,))] if count else []),
        compiler_params=pltpu.CompilerParams(vmem_limit_bytes=limit),
        name=name,
    )(*operands, *[array for array, _, _ in carry], *tokens)


def swaps(pairs):
    return [p for a, b in pairs for p in ((a, b), (b, a))]


def inner_swap(value):
    count = lax.axis_size(AXES)
    return lax.ppermute(value, AXES, swaps([(2 * k, 2 * k + 1) for k in range(count // 2)]))


def outer_swap(value):
    count = lax.axis_size(AXES)
    return lax.ppermute(value, AXES, swaps([(2 * k + 1, 2 * k + 2) for k in range(count // 2 - 1)]))


def exchange(pair_edge, chip_edge):
    return inner_swap(pair_edge), outer_swap(chip_edge)


def side(tiles, distance, vector, source=None, columns=None):
    entry = dict(tiles=tiles, distance=distance, vector=vector)
    if source is not None:
        entry.update(source=source, columns=columns)
    return entry


def on_device(
    pulse_rhs, blocks_fine, columns_fine, aggregate_fine, blocks_mid, columns_mid, aggregate_mid,
    blocks_low, columns_low, aggregate_low, coarse_ops, coarse_maps,
):
    panels, width = pulse_rhs.shape[0], blocks_fine.shape[-1]
    devices = lax.axis_size(AXES)
    blocks = (blocks_fine, blocks_mid, blocks_low)
    columns = (columns_fine.T, columns_mid, columns_low)
    aggregates = tuple(a.reshape(1, -1) for a in (aggregate_fine, aggregate_mid, aggregate_low))
    counts = tuple(b.shape[0] for b in blocks)
    depths = coarse_ops.shape[1]
    wide = (6, 6)
    reach = tuple(w - HALO for w in wide)
    edge_rows = HALO * panels

    def rows(tiles, extra=0):
        return ((tiles * panels + extra, width), F32)

    def vec(level):
        return rows(counts[level])

    def diag(level):
        return ((counts[level], width), F32)

    def ext(level):
        return [pltpu.VMEM((counts[level] + 2 * HALO, 2 * panels, width), BF16)]

    def wide_call(level, finish, layout, shapes, operands, integers, near_pair, near_chip, step):
        operands = dict(
            operands, source=sources[level], diagonal=diagonals[level], blocks=weights if level == 0 else blocks[level], columns=columns[level],
            integers_pair=integers[0], integers_chip=integers[1], blocks_pair=near_pair,
            **{f"blocks_chip{k}": piece for k, piece in enumerate(near_chip)},
        )
        names = tuple(operands)
        count = counts[level] + 2 * wide[level]
        return step(
            f"wide_{finish}{level}", functools.partial(wide_kernel, names, layout, panels, wide[level], integers[2], finish, len(shapes)),
            shapes, tuple(operands[k] for k in names),
            scalars=tuple(k for k, name in enumerate(names) if "columns" in name),
            remote=tuple(k for k, name in enumerate(names) if name.startswith(("integers", "blocks_"))),
            scratch=[pltpu.VMEM((count, 2 * panels, width), BF16)] * 2
            + [pltpu.VMEM((count * panels, width), F32)] * 2
            + [
                pltpu.VMEM((2 * reach[level], 8, width), F32),
                pltpu.VMEM((2, reach[level]) + blocks_fine.shape[1:], F32),
                pltpu.SMEM((2, 8, width), F32),
                pltpu.SemaphoreType.DMA((3 + len(near_chip),)),
            ],
        )

    def facing(towards_pair, tile):
        def first():
            core = lax.axis_index("pair")
            return (1 - core if towards_pair else core) * (counts[0] - reach[0]) + tile
        return first

    pieces_of = {
        **{f"mid{k}": (blocks_mid, k, 1) for k in range(counts[1])},
        **{f"fine{k}": (blocks_fine, facing(False, k), 1) for k in range(reach[0])},
    }
    arrived = {}

    def step(name, kernel, shapes, operands, tokens=(), **more):
        leaving = LEAVE.get(name, ())
        outs = call(
            kernel, shapes, operands, name=name, carry=[pieces_of[p] for p in leaving],
            tokens=[arrived[p] for p in ARRIVE.get(name, ())] + list(tokens), **more,
        )
        pieces = dict(zip(leaving, outs[len(shapes):]))
        return outs[:len(shapes)], lambda: arrived.update({p: outer_swap(v) for p, v in pieces.items()})

    mid_pair = inner_swap(blocks_mid)
    images = call(maps_kernel, [((width // 2, 2 * depths * width), BF16)], (coarse_ops, coarse_maps), name="maps")[0]

    first_edge = rows(HALO + reach[0], 8)
    (diagonal, vector, pair_edge, chip_edge), leave = step(
        "first", functools.partial(first_kernel, reach[0]), [diag(0), vec(0), first_edge, first_edge],
        (columns[0], pulse_rhs, blocks_fine), scalars=(0,), remote=(2,), scratch=[pltpu.VMEM(blocks_fine.shape, F32), pltpu.SemaphoreType.DMA((4,))],
    )
    sources, diagonals = [pulse_rhs], [diagonal]
    halos = first_halos = exchange(pair_edge, chip_edge)
    leave()
    links = blocks_fine.shape[1]
    weights = call(
        prepare_kernel, [((counts[0], links * width, 2 * width), BF16)], (blocks_fine,), remote=(0,),
        scratch=[pltpu.VMEM(blocks_fine.shape, F32), pltpu.SemaphoreType.DMA((4,))], name="prepare",
    )[0]
    for k in range(2):
        (vector, pair_edge, chip_edge), leave = step(
            f"sweep0{k}", functools.partial(sweep_kernel, panels, True), [vec(0), rows(HALO), rows(HALO)],
            (columns[0], vector, *halos, pulse_rhs, diagonal, weights), scalars=(0,), scratch=ext(0),
        )
        halos = exchange(pair_edge, chip_edge)
        leave()
    kept = [vector]
    fine_pair = call(copy_kernel, [], (), name="near", carry=[(blocks_fine, facing(True, 0), reach[0])])[0]
    fine_pair = inner_swap(fine_pair)
    (source, diagonal, vector, packed), leave = step(
        "residual0", functools.partial(residual_kernel, panels),
        [vec(1), diag(1), vec(1), rows(2 * counts[1] + HALO, 8)],
        (columns[0], vector, *halos, pulse_rhs, weights, aggregates[0], columns_mid, blocks_mid),
        scalars=(0, 7), scratch=ext(0),
    )
    sources.append(source)
    diagonals.append(diagonal)

    size = counts[1] * panels
    pair = inner_swap(packed)
    chip = outer_swap(jnp.concatenate([packed[:2 * size + 8], pair[2 * size + 8:]]))
    leave()
    far = inner_swap(chip[:size])
    first_mid = (pair, chip, 2 * size)

    def mid_layout(second):
        return {
            "out": [side(counts[1], 1, ("chip", 0), ("chip_source", size), (1, 0)), side(HALO, 1, ("chip", second))],
            "in": [side(counts[1], 1, ("pair", 0), ("pair_source", size), (0, 0)), side(HALO, 1, ("far", "core"))],
        }

    mid_chip = [arrived[f"mid{k}"] for k in range(counts[1])]
    (vector, source, diagonal, next_vector), leave = wide_call(
        1, "down", mid_layout(2 * size + 8), [vec(1), vec(2), diag(2), vec(2)],
        dict(vector=vector, pair=pair, chip=chip, far=far, pair_source=pair, chip_source=chip,
             aggregate=aggregates[1], next_columns=columns_low, next_blocks=blocks_low),
        first_mid, mid_pair, mid_chip, step,
    )
    kept.append(vector)
    sources.append(source)
    diagonals.append(diagonal)

    vector = next_vector
    halos = exchange(vector, vector)
    leave()

    def sweep_low(name, vector, halos):
        (vector,), leave = step(
            name, functools.partial(sweep_kernel, panels, False), [vec(2)],
            (columns_low, vector, *halos, sources[2], diagonals[2], blocks_low), scalars=(0,), scratch=ext(2),
        )
        halos = exchange(vector, vector)
        leave()
        return vector, halos

    for k in range(2):
        vector, halos = sweep_low(f"down2{k}", vector, halos)
    (own_piece, outgoing), _ = step(
        "lowest", functools.partial(lowest_kernel, panels),
        [((panels, width), F32), ((devices, panels // 2, width), F32)],
        (columns_low, vector, *halos, sources[2], blocks_low, aggregates[2], images),
        scalars=(0,), scratch=ext(2), tokens=[fine_pair],
    )
    incoming = lax.all_to_all(outgoing, AXES, 0, 0)
    (vector,), leave = step(
        "chain", functools.partial(chain_kernel, panels), [vec(2)],
        (own_piece, incoming, coarse_ops, coarse_maps, aggregates[2], vector),
    )
    halos = exchange(vector, vector)
    leave()
    for k in range(2):
        vector, halos = sweep_low(f"up2{k}", vector, halos)
    (vector, packed), leave = step(
        "prolong2", functools.partial(prolong_kernel, panels), [vec(1), rows(counts[1] + HALO)],
        (columns_low, vector, *halos, sources[2], diagonals[2], blocks_low, aggregates[1], kept[1]),
        scalars=(0,), scratch=ext(2),
    )

    pair = inner_swap(packed)
    chip = outer_swap(jnp.concatenate([vector, pair[size:]]))
    leave()
    far = inner_swap(chip[:size])
    (vector, pair_edge, chip_edge), leave = wide_call(
        1, "up", mid_layout(size), [vec(0), rows(wide[0]), rows(wide[0])],
        dict(vector=vector, pair=pair, chip=chip, far=far, pair_source=first_mid[0], chip_source=first_mid[1],
             aggregate=aggregates[0], upper=kept[0]),
        first_mid, mid_pair, mid_chip, step,
    )

    pair, chip = exchange(pair_edge, chip_edge)
    layout = {
        name: [side(reach[0], 1, (array, 0), (array + "_source", edge_rows + 8), (which, 0)),
               side(HALO, 1, (array, reach[0] * panels))]
        for name, array, which in (("out", "chip", 1), ("in", "pair", 0))
    }
    return wide_call(
        0, "last", layout, [(pulse_rhs.shape, F32)],
        dict(vector=vector, pair=pair, chip=chip, pair_source=first_halos[0], chip_source=first_halos[1]),
        (*first_halos, edge_rows), fine_pair, [arrived[f"fine{k}"] for k in range(reach[0])], step,
    )[0][0]


LEAVE = {'first': ('mid0', 'mid1'), 'sweep00': ('mid2',), 'sweep01': ('mid3',), 'down20': ('fine0',), 'chain': ('fine1',), 'up20': ('fine2',), 'up21': ('fine3',)}
ARRIVE = {'sweep01': ('mid0', 'mid1'), 'residual0': ('mid2',), 'lowest': ('fine0',), 'up21': ('fine1',), 'prolong2': ('fine2',)}


def solution(mesh):
    split_first = P(AXES)
    rhs = P(None, AXES)
    return jax.shard_map(
        on_device, mesh=mesh, in_specs=(rhs,) + (split_first,) * 11, out_specs=rhs, check_vma=False
    )
```
